32 devices in a mesh: dp: 16 (over z, x, core), fsdp: 2 (over y).
Axes of the slice: x: 2, y: 2, z: 4, core: 2. Of those that a mesh axis runs over, the one named last changes fastest.
Arguments:
- query_rows: bfloat16 [4096, 2048], P(('dp', 'fsdp')), may hold values from -12 to 12
- key_rows: bfloat16 [4096, 2048], P(('dp', 'fsdp')), may hold values from -12 to 12
- value_rows: bfloat16 [4096, 2048], P(('dp', 'fsdp')), may hold values from -6 to 6
- out_grad: bfloat16 [4096, 2048], P(('dp', 'fsdp')), may hold values from -6 to 6
- params: float32 [32768, 2048], P(('dp', 'fsdp')), may hold values from -6 to 6
- momentum: float32 [32768, 2048], P(('dp', 'fsdp')), may hold values from -3 to 3
- token_ids: int32 [4096], P(('dp', 'fsdp')), may hold values from 0 to 8191
- block_mask: int32 [2, 2], replicated, may hold values from 0 to 1, as said below
- step_index: int32 [1], replicated, may hold values from 0 to 7
Outputs:
- grad_query: bfloat16 [4096, 2048], P(('dp', 'fsdp'))
- grad_key: bfloat16 [4096, 2048], P(('dp', 'fsdp'))
- grad_value: bfloat16 [4096, 2048], P(('dp', 'fsdp'))
- new_params: float32 [32768, 2048], P(('dp', 'fsdp'))
- new_momentum: float32 [32768, 2048], P(('dp', 'fsdp'))
The draws below stay inside these ranges and needn't reach their ends.
Inputs may be any that keep to these rules, and one draw needn't show every extreme that they name: block_mask[i, i] is 1 and block_mask[i, j] is 0 for j > i.
All inputs are finite; a program needn't handle non-finite values.
Results may differ from the reference program's by a relative error of at most 0.0095.
Values may be sent and summed in bfloat16 or wider, within the bound.
No kernel may reach another device: no remote copies, remote signals or barrier semaphores. Data moves between devices by JAX's collectives and lax.ppermute only.
A program may use at most 128 MiB of HBM per device.

```python
import math
import jax
import jax.numpy as jnp
from jax import lax

D = 2048
HEADS = 16
HD = 128
STEMS = 4
CODES = 2048
BLOCK = 128
INNER = 2048
TOKENS = 256
NB = 2
ALL_TOKENS = 4096
ALL_INNER = 32768
N_DP = 16


def paired_rows(key):
    base_key = jax.random.fold_in(key, 7301)
    query_part = jnp.clip(jax.random.normal(jax.random.fold_in(base_key, 1), (ALL_TOKENS, INNER), jnp.float32), -6.0, 6.0)
    key_part = jnp.clip(jax.random.normal(jax.random.fold_in(base_key, 2), (ALL_TOKENS, INNER), jnp.float32), -6.0, 6.0)
    return (query_part, key_part)


def draw_query_rows(key, part):
    return paired_rows(key)[0].astype(jnp.bfloat16)


def draw_key_rows(key, part):
    return paired_rows(key)[1].astype(jnp.bfloat16)


def draw_block_mask(key, part):
    coin_flips = jax.random.randint(jax.random.fold_in(key, 4409), (NB, NB), 0, 2, dtype=jnp.int32)
    row_index = jnp.arange(NB, dtype=jnp.int32)[:, None]
    col_index = jnp.arange(NB, dtype=jnp.int32)[None, :]
    return jnp.where(row_index == col_index, 1, jnp.where(col_index < row_index, coin_flips, 0)).astype(jnp.int32)


def place_ends(values, own_key, smallest, top_value):
    dims = values.shape
    spot = [jax.random.randint(jax.random.fold_in(own_key, axis), (), 0, dims[axis]) for axis in range(len(dims))]
    values = values.at[tuple(spot)].set(smallest)
    longest = dims.index(max(dims))
    spot[longest] = (spot[longest] + 1) % dims[longest]
    return values.at[tuple(spot)].set(top_value)


def levels(rng, dims, cuts, smallest, top_value):
    def one(dim, parts):
        draws = jax.random.uniform(jax.random.fold_in(jax.random.fold_in(rng, 6), dim), (parts,), jnp.float32, smallest / len(cuts), top_value / len(cuts))
        return jnp.repeat(jnp.exp(draws), dims[dim] // parts).reshape((-1,) + (1,) * (len(dims) - dim - 1))

    loudness = one(*cuts[0])
    for cut in cuts[1:]:
        loudness = loudness * one(*cut)
    return loudness


def centred(stream_key, extent, deviation, bound, cuts=(), kind=jnp.bfloat16):
    factor_of = levels(stream_key, extent, cuts, -0.22, 0.18) if cuts else 1.0
    drawn = jax.random.normal(stream_key, extent, jnp.float32) * deviation * factor_of
    return jnp.minimum(jnp.maximum(drawn, -bound), bound).astype(kind)


def setup_inputs(seed: int = 0) -> dict:
    streams_of = jax.random.split(jax.random.key(seed), 10)
    query_rows = draw_query_rows(jax.random.fold_in(streams_of[9], 71), 0)
    key_rows = draw_key_rows(jax.random.fold_in(streams_of[9], 71), 0)
    value_rows = centred(streams_of[2], (ALL_TOKENS, INNER), 1.0, 6.0, ((0, 32),))
    out_grad = centred(streams_of[3], (ALL_TOKENS, D), 1.0, 6.0, ((0, 32),))
    params = centred(streams_of[4], (ALL_INNER, D), 1.0, 6.0, ((0, 32),), jnp.float32)
    momentum = centred(streams_of[5], (ALL_INNER, D), 0.5, 3.0, ((0, 32),), jnp.float32)
    token_ids = place_ends(jax.random.randint(streams_of[6], (ALL_TOKENS,), 0, STEMS * CODES), jax.random.fold_in(streams_of[6], 1), 0, (STEMS * CODES) - 1).astype(jnp.int32)
    block_mask = draw_block_mask(jax.random.fold_in(streams_of[9], 71), 0)
    step_index = jax.random.randint(streams_of[8], (1,), 0, 8).astype(jnp.int32)
    return {"query_rows": query_rows, "key_rows": key_rows, "value_rows": value_rows, "out_grad": out_grad, "params": params, "momentum": momentum, "token_ids": token_ids, "block_mask": block_mask, "step_index": step_index}


MOMENTUM_RATE = 0.9
LEARN_RATE = 0.25

def rounded(values):
    return lax.optimization_barrier(values.astype(jnp.bfloat16)).astype(jnp.float32)

def replica_step(query_rows, key_rows, value_rows, out_grad, params, momentum, token_ids, block_mask, step_value):
    inv_width = 1.0 / math.sqrt(INNER)
    score_scale = 1.0 / math.sqrt(HD)
    weight16 = rounded(params)
    grad_out32 = out_grad.astype(jnp.float32)
    grad_attn = rounded(jnp.dot(grad_out32, weight16.T, preferred_element_type=jnp.float32) * inv_width)
    position = jnp.arange(TOKENS, dtype=jnp.int32)
    block_of = position // BLOCK
    spread = block_mask[block_of[:, None], block_of[None, :]]
    stem_ids = token_ids // CODES
    allowed = (spread == 1) & (position[None, :] <= position[:, None]) & ((stem_ids[:, None] == stem_ids[None, :]) | (block_of[:, None] == block_of[None, :]))
    query_h = query_rows.astype(jnp.float32).reshape(TOKENS, HEADS, HD)
    key_h = key_rows.astype(jnp.float32).reshape(TOKENS, HEADS, HD)
    value_h = value_rows.astype(jnp.float32).reshape(TOKENS, HEADS, HD)
    grad_h = grad_attn.reshape(TOKENS, HEADS, HD)
    scores = jnp.einsum('qhd,khd->hqk', query_h, key_h) * score_scale
    scores = jnp.where(allowed[None], scores, -1e+30)
    top_score = lax.optimization_barrier(jnp.max(scores, axis=-1, keepdims=True))
    exp_terms = jnp.where(allowed[None], jnp.exp(scores - top_score), 0.0)
    prob_f32 = exp_terms / lax.optimization_barrier(jnp.sum(exp_terms, axis=-1, keepdims=True))
    prob_b16 = rounded(prob_f32)
    attended = rounded(jnp.einsum('hqk,khd->qhd', prob_b16, value_h)).reshape(TOKENS, INNER)
    grad_value = jnp.einsum('hqk,qhd->khd', prob_b16, grad_h).reshape(TOKENS, INNER)
    grad_prob = jnp.einsum('qhd,khd->hqk', grad_h, value_h)
    row_dot = lax.optimization_barrier(jnp.sum(prob_f32 * grad_prob, axis=-1, keepdims=True))
    grad_score = rounded(prob_f32 * (grad_prob - row_dot) * score_scale)
    grad_query = jnp.einsum('hqk,khd->qhd', grad_score, key_h).reshape(TOKENS, INNER)
    grad_key = jnp.einsum('hqk,qhd->khd', grad_score, query_h).reshape(TOKENS, INNER)
    grad_weight = jnp.dot(attended.T, grad_out32, preferred_element_type=jnp.float32) * inv_width
    moment = MOMENTUM_RATE * momentum + grad_weight
    correction = 1.0 / (1.0 - jnp.exp((step_value + 1).astype(jnp.float32) * math.log(MOMENTUM_RATE)))
    stepped = params - LEARN_RATE * correction * moment
    return (grad_query.astype(jnp.bfloat16), grad_key.astype(jnp.bfloat16), grad_value.astype(jnp.bfloat16), stepped, moment)

def reference(query_rows, key_rows, value_rows, out_grad, params, momentum, token_ids, block_mask, step_index):
    step_value = step_index[0]

    def per_replica(pieces):
        return replica_step(pieces[0], pieces[1], pieces[2], pieces[3], pieces[4], pieces[5], pieces[6], block_mask, step_value)
    stacked = (query_rows.reshape(N_DP, TOKENS, INNER), key_rows.reshape(N_DP, TOKENS, INNER), value_rows.reshape(N_DP, TOKENS, INNER), out_grad.reshape(N_DP, TOKENS, D), params.reshape(N_DP, INNER, D), momentum.reshape(N_DP, INNER, D), token_ids.reshape(N_DP, TOKENS))
    grad_query, grad_key, grad_value, stepped, moment = lax.map(per_replica, stacked)
    replica_ids = jnp.arange(N_DP, dtype=jnp.int32)
    partner = jnp.bitwise_xor(replica_ids, jnp.left_shift(jnp.int32(1), step_value % 4)).astype(jnp.int32)
    new_params = 0.5 * (stepped + stepped[partner])
    new_momentum = 0.5 * (moment + moment[partner])
    return (grad_query.reshape(ALL_TOKENS, INNER), grad_key.reshape(ALL_TOKENS, INNER), grad_value.reshape(ALL_TOKENS, INNER), new_params.reshape(ALL_INNER, D), new_momentum.reshape(ALL_INNER, D))
```

```python
import functools
import math

import jax
import jax.numpy as jnp
from jax import lax
from jax.experimental import pallas as pl
from jax.experimental.pallas import tpu as pltpu
from jax.sharding import PartitionSpec as P

HD = 128
CODES = 2048
MOMENTUM_RATE = 0.9
LEARN_RATE = 0.25
MIB = 1 << 20

CONTRACT_LAST = (((1,), (1,)), ((), ()))
CONTRACT_FIRST = (((0,), (0,)), ((), ()))


def dot_f32(left, right, dims):
    return lax.dot_general(left, right, dims, preferred_element_type=jnp.float32)


def params_of(limit):
    return pltpu.CompilerParams(vmem_limit_bytes=limit)


def row_chunks(rows):
    sizes, left = [], rows
    while left > 2 * HD:
        sizes.append(min(2 * HD, left - 2 * HD))
        left -= sizes[-1]
    return sizes + [HD] * (left // HD)


def chunk_starts(sizes):
    starts, at = [], 0
    for size in sizes:
        starts.append(at)
        at += size
    return starts


def partner_route(count, bit_level):
    route = []
    for low in range(count):
        high = low | 1 << bit_level
        if high != low and high < count:
            route += [(low, high), (high, low)]
    return route


def shift_route(count, shift):
    return [(source, (source + shift) % count) for source in range(count)]


def short_rows(params, start, size):
    width = params.shape[1]
    step = math.gcd(size, 64)

    def body(wide_ref, short_ref):
        short_ref[...] = wide_ref[...].astype(jnp.bfloat16)

    return pl.pallas_call(
        body,
        grid=(size // step,),
        in_specs=[pl.BlockSpec((step, width), lambda i: (start // step + i, 0))],
        out_specs=pl.BlockSpec((step, width), lambda i: (i, 0)),
        out_shape=jax.ShapeDtypeStruct((size, width), jnp.bfloat16),
        compiler_params=params_of(8 * MIB),
        cost_estimate=pl.CostEstimate(
            flops=size * width, bytes_accessed=6 * size * width, transcendentals=0
        ),
        name="short_rows",
    )(params)


def packed_heads(place, query_rows, key_rows, value_rows, shift, count):
    rows, width = query_rows.shape
    local = width // count

    def body(place_ref, query_ref, key_ref, value_ref, pack_ref):
        pack_ref[0] = query_ref[...]
        pack_ref[1] = key_ref[...]
        pack_ref[2] = value_ref[...]

    spec = pl.BlockSpec(
        (rows, local), lambda i, place_ref: (0, lax.rem(place_ref[0] + shift, count))
    )
    return pl.pallas_call(
        body,
        grid_spec=pltpu.PrefetchScalarGridSpec(
            num_scalar_prefetch=1,
            grid=(1,),
            in_specs=[spec] * 3,
            out_specs=pl.BlockSpec((3, rows, local), lambda i, place_ref: (0, 0, 0)),
        ),
        out_shape=jax.ShapeDtypeStruct((3, rows, local), query_rows.dtype),
        compiler_params=params_of(8 * MIB),
        cost_estimate=pl.CostEstimate(
            flops=0, bytes_accessed=12 * rows * local, transcendentals=0
        ),
        name="packed_heads",
    )(place, query_rows, key_rows, value_rows)


def attention_step(
    place, bias, own_rows, packs, own_grad, far_grads, params, count, together
):
    rows, width = own_rows[0].shape
    local = width // count
    tokens = rows * count
    heads = local // HD
    span = together * HD
    steps = heads // together
    score_scale = 1.0 / math.sqrt(HD)
    inv_width = 1.0 / math.sqrt(width)
    far = count - 1

    def body(place_ref, bias_ref, query_ref, key_ref, value_ref, *refs):
        pack_refs, refs = refs[:far], refs[far:]
        own_grad_ref, refs = refs[0], refs[1:]
        far_refs, refs = refs[:far], refs[far:]
        params_ref, attended_ref, dq_ref, dk_ref, dv_ref, *refs = refs
        back_refs, grads_ref = refs[:far], refs[far]

        @pl.when(pl.program_id(0) == 0)
        def _():
            grads_ref[:rows, :] = own_grad_ref[...]
            for s in range(far):
                grads_ref[(s + 1) * rows : (s + 2) * rows, :] = far_refs[s][...]

        weight = params_ref[...].astype(jnp.bfloat16)
        grad_heads = (dot_f32(grads_ref[...], weight, CONTRACT_LAST) * inv_width).astype(
            jnp.bfloat16
        )
        for g in range(together):
            cols = slice(g * HD, (g + 1) * HD)

            def whole(own_ref, part):
                return jnp.concatenate(
                    [own_ref[:, cols]] + [ref[part, :, cols] for ref in pack_refs], axis=0
                )

            query, key, value = whole(query_ref, 0), whole(key_ref, 1), whole(value_ref, 2)
            grad = grad_heads[:, cols]
            scores = dot_f32(query, key, CONTRACT_LAST) * score_scale + bias_ref[...]
            top = jnp.max(scores, axis=-1, keepdims=True)
            terms = jnp.exp(scores - top)
            prob = terms * (1.0 / jnp.sum(terms, axis=-1, keepdims=True))
            prob16 = prob.astype(jnp.bfloat16)
            attended_ref[:, cols] = jnp.dot(
                prob16, value, preferred_element_type=jnp.float32
            ).astype(jnp.bfloat16)
            grad_value = dot_f32(prob16, grad, CONTRACT_FIRST).astype(jnp.bfloat16)
            grad_prob = dot_f32(grad, value, CONTRACT_LAST)
            row_dot = jnp.sum(prob * grad_prob, axis=-1, keepdims=True)
            grad_score = (prob * (grad_prob - row_dot) * score_scale).astype(jnp.bfloat16)
            grad_query = jnp.dot(
                grad_score, key, preferred_element_type=jnp.float32
            ).astype(jnp.bfloat16)
            grad_key = dot_f32(grad_score, query, CONTRACT_FIRST).astype(jnp.bfloat16)
            for part, (out_ref, result) in enumerate(
                ((dq_ref, grad_query), (dk_ref, grad_key), (dv_ref, grad_value))
            ):
                out_ref[:, cols] = result[:rows]
                for s in range(far):
                    back_refs[s][part, :, cols] = result[(s + 1) * rows : (s + 2) * rows]

    own_spec = pl.BlockSpec(
        (rows, span), lambda i, place_ref: (0, place_ref[0] * steps + i)
    )
    pack_spec = pl.BlockSpec((3, rows, span), lambda i, place_ref: (0, 0, i))
    grad_spec = pl.BlockSpec((rows, width), lambda i, place_ref: (0, 0))
    depth = params.shape[1]
    own_shape = jax.ShapeDtypeStruct((rows, width), jnp.bfloat16)
    macs = tokens * depth * local + 5 * heads * tokens * tokens * HD
    return pl.pallas_call(
        body,
        grid_spec=pltpu.PrefetchScalarGridSpec(
            num_scalar_prefetch=1,
            grid=(steps,),
            in_specs=[pl.BlockSpec((tokens, tokens), lambda i, place_ref: (0, 0))]
            + [own_spec] * 3
            + [pack_spec] * far
            + [grad_spec] * (1 + far)
            + [pl.BlockSpec((span, depth), lambda i, place_ref: (i, 0))],
            out_specs=[pl.BlockSpec((tokens, span), lambda i, place_ref: (0, i))]
            + [own_spec] * 3
            + [pack_spec] * far,
            scratch_shapes=[pltpu.VMEM((tokens, depth), jnp.bfloat16)],
        ),
        out_shape=[jax.ShapeDtypeStruct((tokens, local), jnp.bfloat16)]
        + [own_shape] * 3
        + [jax.ShapeDtypeStruct((3, rows, local), jnp.bfloat16)] * far,
        compiler_params=params_of((24 if tokens <= 256 else 56) * MIB),
        cost_estimate=pl.CostEstimate(
            flops=2 * macs,
            bytes_accessed=4 * local * depth + 16 * tokens * local,
            transcendentals=heads * tokens * tokens,
        ),
        name="attention_step",
    )(place, bias, *own_rows, *packs, own_grad, *far_grads, params)


def moment_rows(attended, own_grad, far_grads, momentum, start, size, local):
    rows, depth = own_grad.shape
    far = len(far_grads)
    tokens = attended.shape[0]
    step = math.gcd(size, HD)
    first = start // step
    inv_width = 1.0 / math.sqrt(local * (far + 1))

    def body(attended_ref, own_ref, *refs):
        far_refs, (momentum_ref, moment_ref) = refs[:far], refs[far:]
        total = dot_f32(attended_ref[:rows, :], own_ref[...], CONTRACT_FIRST)
        for s in range(far):
            total += dot_f32(
                attended_ref[(s + 1) * rows : (s + 2) * rows, :],
                far_refs[s][...],
                CONTRACT_FIRST,
            )
        moment_ref[...] = (
            MOMENTUM_RATE * momentum_ref[...] + total * inv_width
        ).astype(jnp.bfloat16)

    grad_spec = pl.BlockSpec((rows, depth), lambda i: (0, 0))
    return pl.pallas_call(
        body,
        grid=(size // step,),
        in_specs=[pl.BlockSpec((tokens, step), lambda i: (0, first + i))]
        + [grad_spec] * (1 + far)
        + [pl.BlockSpec((step, depth), lambda i: (first + i, 0))],
        out_specs=pl.BlockSpec((step, depth), lambda i: (i, 0)),
        out_shape=jax.ShapeDtypeStruct((size, depth), jnp.bfloat16),
        compiler_params=params_of(24 * MIB),
        cost_estimate=pl.CostEstimate(
            flops=2 * tokens * size * depth,
            bytes_accessed=6 * size * depth + 2 * tokens * depth,
            transcendentals=0,
        ),
        name="moment_rows",
    )(attended, own_grad, *far_grads, momentum)


def averaged_rows(rate, params, far_params, moment, far_moment, start, size, results):
    depth = params.shape[1]
    step = math.gcd(size, 32)
    first = start // step

    def body(rate_ref, params_ref, far_params_ref, moment_ref, far_moment_ref, *refs):
        new_params_ref, new_momentum_ref = refs[-2:]
        mean_moment = 0.5 * (
            moment_ref[...].astype(jnp.float32) + far_moment_ref[...].astype(jnp.float32)
        )
        mean_params = 0.5 * (params_ref[...] + far_params_ref[...].astype(jnp.float32))
        new_momentum_ref[...] = mean_moment
        new_params_ref[...] = mean_params - rate_ref[0] * mean_moment

    whole_spec = pl.BlockSpec((step, depth), lambda i: (first + i, 0))
    part_spec = pl.BlockSpec((step, depth), lambda i: (i, 0))
    kept = [] if results is None else list(results)
    return pl.pallas_call(
        body,
        grid=(size // step,),
        in_specs=[
            pl.BlockSpec(memory_space=pltpu.SMEM),
            whole_spec,
            part_spec,
            part_spec,
            part_spec,
        ]
        + [pl.BlockSpec(memory_space=pl.ANY)] * len(kept),
        out_specs=[whole_spec] * 2,
        out_shape=[jax.ShapeDtypeStruct(params.shape, jnp.float32)] * 2,
        input_output_aliases={5 + i: i for i in range(len(kept))},
        compiler_params=params_of(8 * MIB),
        cost_estimate=pl.CostEstimate(
            flops=6 * size * depth, bytes_accessed=18 * size * depth, transcendentals=0
        ),
        name="averaged_rows",
    )(rate, params, far_params, moment, far_moment, *kept)


def placed_heads(place, packs, results):
    count = len(packs) + 1
    rows, width = results[0].shape
    local = width // count
    for shift, pack in enumerate(packs, 1):

        def body(place_ref, pack_ref, *refs):
            for part in range(3):
                refs[3 + part][...] = pack_ref[part]

        spec = pl.BlockSpec(
            (rows, local),
            lambda i, place_ref, shift=shift: (0, lax.rem(place_ref[0] + shift, count)),
        )
        results = pl.pallas_call(
            body,
            grid_spec=pltpu.PrefetchScalarGridSpec(
                num_scalar_prefetch=1,
                grid=(1,),
                in_specs=[pl.BlockSpec((3, rows, local), lambda i, place_ref: (0, 0, 0))]
                + [pl.BlockSpec(memory_space=pl.ANY)] * 3,
                out_specs=[spec] * 3,
            ),
            out_shape=[jax.ShapeDtypeStruct((rows, width), jnp.bfloat16)] * 3,
            input_output_aliases={2 + part: part for part in range(3)},
            compiler_params=params_of(8 * MIB),
            cost_estimate=pl.CostEstimate(
                flops=0, bytes_accessed=12 * rows * local, transcendentals=0
            ),
            name="placed_heads",
        )(place, pack, *results)
    return results


def score_bias(me, count, own_ids, far_ids, block_mask):
    rows = own_ids.shape[0]
    blocks = block_mask.shape[0]
    block_rows = rows * count // blocks
    stems = jnp.concatenate([own_ids] + far_ids) // CODES
    position = jnp.concatenate(
        [lax.rem(me + count - s, count) * rows + jnp.arange(rows) for s in range(count)]
    )
    block_of = position // block_rows
    picks = (block_of[:, None] == jnp.arange(blocks)[None, :]).astype(jnp.float32)
    spread = jnp.dot(jnp.dot(picks, block_mask.astype(jnp.float32)), picks.T)
    allowed = (
        (spread > 0.5)
        & (position[None, :] <= position[:, None])
        & ((stems[:, None] == stems[None, :]) | (block_of[:, None] == block_of[None, :]))
    )
    return jnp.where(allowed, 0.0, -1e30)


def step_with_partner(
    bit_level,
    query_rows,
    key_rows,
    value_rows,
    out_grad,
    params,
    momentum,
    token_ids,
    block_mask,
    rate,
):
    count = lax.axis_size("fsdp")
    me = lax.axis_index("fsdp")
    place = me.astype(jnp.int32).reshape(1)
    local = params.shape[0]
    route = partner_route(lax.axis_size("dp"), bit_level)
    sizes = row_chunks(local)
    starts = chunk_starts(sizes)
    chunks = list(zip(starts, sizes))

    far_ids, far_grads, packs = [], [], []
    for shift in range(1, count):
        ring = shift_route(count, shift)
        far_ids.append(lax.ppermute(token_ids, "fsdp", ring))
        far_grads.append(lax.ppermute(out_grad, "fsdp", ring))
        pack = packed_heads(place, query_rows, key_rows, value_rows, shift, count)
        packs.append(lax.ppermute(pack, "fsdp", ring))
    far_params = [None] * len(chunks)
    for at in reversed(range(len(chunks))):
        start, size = chunks[at]
        far_params[at] = lax.ppermute(short_rows(params, start, size), "dp", route)

    bias = score_bias(me, count, token_ids, far_ids, block_mask)
    heads = local // HD
    attended, *grads = attention_step(
        place,
        bias,
        (query_rows, key_rows, value_rows),
        packs,
        out_grad,
        far_grads,
        params,
        count,
        math.gcd(heads, 2),
    )
    results, backs = grads[:3], grads[3:]
    returned = [
        lax.ppermute(back, "fsdp", shift_route(count, -shift))
        for shift, back in enumerate(backs, 1)
    ]
    moments = [
        moment_rows(attended, out_grad, far_grads, momentum, start, size, local)
        for start, size in chunks
    ]
    far_moments = [lax.ppermute(moment, "dp", route) for moment in moments]
    means = None
    for at, (start, size) in enumerate(chunks):
        means = averaged_rows(
            rate, params, far_params[at], moments[at], far_moments[at], start, size, means
        )
    results = placed_heads(place, returned, results)
    return (*results, *means)


def shards(
    query_rows, key_rows, value_rows, out_grad, params, momentum, token_ids, block_mask, step_index
):
    step_value = step_index[0]
    correction = 1.0 / (
        1.0 - jnp.exp((step_value + 1).astype(jnp.float32) * math.log(MOMENTUM_RATE))
    )
    rate = (LEARN_RATE * correction).reshape(1)
    return lax.switch(
        step_value % 4,
        [functools.partial(step_with_partner, bit_level) for bit_level in range(4)],
        query_rows,
        key_rows,
        value_rows,
        out_grad,
        params,
        momentum,
        token_ids,
        block_mask,
        rate,
    )


def solution(mesh):
    rows = P(("dp", "fsdp"), None)
    return jax.shard_map(
        shards,
        mesh=mesh,
        in_specs=(rows,) * 6 + (P(("dp", "fsdp")), P(), P()),
        out_specs=(rows,) * 5,
        check_vma=False,
    )
```

```python
import functools
import math

import jax
import jax.numpy as jnp
from jax import lax
from jax.experimental import pallas as pl
from jax.experimental.pallas import tpu as pltpu
from jax.sharding import PartitionSpec as P

HD = 128
CODES = 2048
MOMENTUM_RATE = 0.9
LEARN_RATE = 0.25
MIB = 1 << 20

CONTRACT_LAST = (((1,), (1,)), ((), ()))
CONTRACT_FIRST = (((0,), (0,)), ((), ()))


def dot_f32(left, right, dims):
    return lax.dot_general(left, right, dims, preferred_element_type=jnp.float32)


def cost_of(macs, moved):
    return pl.CostEstimate(flops=2 * macs, bytes_accessed=moved, transcendentals=0)


def params_of(limit):
    return pltpu.CompilerParams(vmem_limit_bytes=limit)


def row_chunks(start, rows):
    chunks, end = [], start + rows
    while start < end:
        left = (end - start) // HD
        size = HD * (left // 2 if left > 2 else 1)
        chunks.append((start, size))
        start += size
    return chunks


def in_hbm(array):
    return pltpu.with_memory_space_constraint(array, pltpu.HBM)


def partner_route(count, bit_level):
    route = []
    for low in range(count):
        high = low | 1 << bit_level
        if high != low and high < count:
            route += [(low, high), (high, low)]
    return route


def shift_route(count, shift):
    return [(source, (source + shift) % count) for source in range(count)]


def short_rows(params, start, size):
    width = params.shape[1]
    step = math.gcd(size, 64)

    def body(wide_ref, short_ref):
        short_ref[...] = wide_ref[...].astype(jnp.bfloat16)

    return pl.pallas_call(
        body,
        grid=(size // step,),
        in_specs=[pl.BlockSpec((step, width), lambda i: (start // step + i, 0))],
        out_specs=pl.BlockSpec((step, width), lambda i: (i, 0)),
        out_shape=jax.ShapeDtypeStruct((size, width), jnp.bfloat16),
        compiler_params=params_of(8 * MIB),
        cost_estimate=cost_of(0, 6 * size * width),
        name="short_rows",
    )(params)


def packed_heads(place, tensors, out_grad, token_ids, shift, count, group, groups):
    rows, width = tensors[0].shape
    span = width // count // groups
    slabs = out_grad.shape[1] // span if group == 0 else 0

    def body(place_ref, query_ref, key_ref, value_ref, *refs):
        pack_ref = refs[-2] if slabs else refs[-1]
        for slab in range(slabs):
            pack_ref[slab] = refs[0][:, slab * span : (slab + 1) * span]
        if slabs:
            refs[-1][...] = refs[1][...]
        pack_ref[slabs] = query_ref[...]
        pack_ref[slabs + 1] = key_ref[...]
        pack_ref[slabs + 2] = value_ref[...]

    spec = pl.BlockSpec(
        (rows, span),
        lambda i, place_ref: (0, lax.rem(place_ref[0] + shift, count) * groups + group),
    )
    grad_spec = pl.BlockSpec(out_grad.shape, lambda i, place_ref: (0, 0))
    ids_spec = pl.BlockSpec((1, rows), lambda i, place_ref: (0, 0))
    outs = pl.pallas_call(
        body,
        grid_spec=pltpu.PrefetchScalarGridSpec(
            num_scalar_prefetch=1,
            grid=(1,),
            in_specs=[spec] * 3
            + [grad_spec, ids_spec] * (slabs > 0),
            out_specs=[
                pl.BlockSpec((slabs + 3, rows, span), lambda i, place_ref: (0, 0, 0))
            ]
            + [ids_spec] * (slabs > 0),
        ),
        out_shape=[jax.ShapeDtypeStruct((slabs + 3, rows, span), out_grad.dtype)]
        + [jax.ShapeDtypeStruct((1, rows), token_ids.dtype)] * (slabs > 0),
        compiler_params=params_of(12 * MIB),
        cost_estimate=cost_of(0, 4 * (slabs + 3) * rows * span),
        name="packed_heads",
    )(place, *tensors, *[out_grad, token_ids.reshape(1, rows)] * (slabs > 0))
    return outs[0], outs[1].reshape(rows) if slabs else None


def attention_step(
    place, bias, tensors, packs, grads, params, results, count, group, groups, short_out
):
    rows, width = tensors[0].shape
    tokens = rows * count
    heads = width // count // HD // groups
    together = math.gcd(heads, 2)
    span = together * HD
    steps = heads // together
    depth = params.shape[1]
    first = group == 0
    slabs = packs[0].shape[0] - 3 if packs else 0
    slab = heads * HD
    kept = [] if results is None else list(results)
    score_scale = 1.0 / math.sqrt(HD)
    inv_width = 1.0 / math.sqrt(width)
    far = count - 1

    def body(place_ref, bias_ref, query_ref, key_ref, value_ref, *refs):
        pack_refs, refs = [refs[3 * s : 3 * s + 3] for s in range(far)], refs[3 * far :]
        slab_refs, refs = refs[: far * first], refs[far * first :]
        grads_ref, params_ref = refs[:2]
        refs = refs[2 + len(kept) :]
        attended_ref, dq_ref, dk_ref, dv_ref = refs[:4]
        back_refs = refs[4 : 4 + far]

        if first:
            own_ref, grads_ref = grads_ref, refs[4 + far]

            @pl.when(pl.program_id(0) == 0)
            def _():
                grads_ref[:rows, :] = own_ref[...]
                for s in range(far):
                    for at in range(slabs):
                        grads_ref[
                            (s + 1) * rows : (s + 2) * rows, at * slab : (at + 1) * slab
                        ] = slab_refs[s][at]

        weight = params_ref[...].astype(jnp.bfloat16)
        if short_out:
            refs[-1][...] = weight
        grad_heads = (dot_f32(grads_ref[...], weight, CONTRACT_LAST) * inv_width).astype(
            jnp.bfloat16
        )
        for g in range(together):
            cols = slice(g * HD, (g + 1) * HD)

            def whole(own_ref, part):
                return jnp.concatenate(
                    [own_ref[:, cols]] + [far_refs[part][:, cols] for far_refs in pack_refs],
                    axis=0,
                )

            query, key, value = whole(query_ref, 0), whole(key_ref, 1), whole(value_ref, 2)
            grad = grad_heads[:, cols]
            scores = dot_f32(query, key, CONTRACT_LAST) * score_scale + bias_ref[...]
            top = jnp.max(scores, axis=-1, keepdims=True)
            terms = jnp.exp(scores - top)
            prob = terms * (1.0 / jnp.sum(terms, axis=-1, keepdims=True))
            prob16 = prob.astype(jnp.bfloat16)
            attended_ref[:, cols] = jnp.dot(
                prob16, value, preferred_element_type=jnp.float32
            ).astype(jnp.bfloat16)
            grad_value = dot_f32(prob16, grad, CONTRACT_FIRST).astype(jnp.bfloat16)
            grad_prob = dot_f32(grad, value, CONTRACT_LAST)
            row_dot = jnp.sum(prob * grad_prob, axis=-1, keepdims=True)
            grad_score = (prob * (grad_prob - row_dot) * score_scale).astype(jnp.bfloat16)
            grad_query = jnp.dot(
                grad_score, key, preferred_element_type=jnp.float32
            ).astype(jnp.bfloat16)
            grad_key = dot_f32(grad_score, query, CONTRACT_FIRST).astype(jnp.bfloat16)
            for part, (out_ref, result) in enumerate(
                ((dq_ref, grad_query), (dk_ref, grad_key), (dv_ref, grad_value))
            ):
                out_ref[:, cols] = result[:rows]
                for s in range(far):
                    back_refs[s][part, :, cols] = result[(s + 1) * rows : (s + 2) * rows]

    own_spec = pl.BlockSpec(
        (rows, span), lambda i, place_ref: (0, (place_ref[0] * groups + group) * steps + i)
    )
    pack_specs = [
        pl.BlockSpec((None, rows, span), lambda i, place_ref, part=part: (part, 0, i))
        for part in range(slabs, slabs + 3)
    ]
    back_spec = pl.BlockSpec((3, rows, span), lambda i, place_ref: (0, 0, i))
    all_spec = pl.BlockSpec((tokens, depth), lambda i, place_ref: (0, 0))
    own_shape = pltpu.HBM((rows, width), jnp.bfloat16)
    macs = tokens * depth * heads * HD + 5 * heads * tokens * tokens * HD
    operands = [place, bias, *tensors]
    for pack in packs:
        operands += [pack] * 3
    in_specs = (
        [pl.BlockSpec((tokens, tokens), lambda i, place_ref: (0, 0))]
        + [own_spec] * 3
        + pack_specs * far
    )
    if first:
        operands += packs
        in_specs += [
            pl.BlockSpec((slabs, rows, slab), lambda i, place_ref: (0, 0, 0))
        ] * far + [pl.BlockSpec((rows, depth), lambda i, place_ref: (0, 0))]
    else:
        in_specs += [all_spec]
    operands += [grads, params]
    in_specs += [pl.BlockSpec((span, depth), lambda i, place_ref: (group * steps + i, 0))]
    aliases = {len(operands) + i: 1 + i for i in range(len(kept))}
    in_specs += [pl.BlockSpec(memory_space=pl.ANY)] * len(kept)
    return pl.pallas_call(
        body,
        grid_spec=pltpu.PrefetchScalarGridSpec(
            num_scalar_prefetch=1,
            grid=(steps,),
            in_specs=in_specs,
            out_specs=[pl.BlockSpec((tokens, span), lambda i, place_ref: (0, i))]
            + [own_spec] * 3
            + [back_spec] * far
            + [all_spec] * first
            + [pl.BlockSpec((span, depth), lambda i, place_ref: (i, 0))] * short_out,
        ),
        out_shape=[jax.ShapeDtypeStruct((tokens, heads * HD), jnp.bfloat16)]
        + [own_shape] * 3
        + [jax.ShapeDtypeStruct((3, rows, heads * HD), jnp.bfloat16)] * far
        + [jax.ShapeDtypeStruct((tokens, depth), jnp.bfloat16)] * first
        + [jax.ShapeDtypeStruct((heads * HD, depth), jnp.bfloat16)] * short_out,
        input_output_aliases=aliases,
        compiler_params=params_of((24 if tokens <= 256 else 56) * MIB),
        cost_estimate=cost_of(macs, heads * HD * (4 * depth + 16 * tokens)),
        name="attention_step",
    )(*operands, *kept)


def moment_rows(attended, grads, momentum, start, size, group_start, inner, gates):
    tokens, depth = grads.shape
    step = math.gcd(size, HD)
    first = start // step
    first_column = (start - group_start) // step
    inv_width = 1.0 / math.sqrt(inner)


    def body(attended_ref, grads_ref, momentum_ref, *refs):
        total = dot_f32(attended_ref[...], grads_ref[...], CONTRACT_FIRST)
        refs[-1][...] = (
            MOMENTUM_RATE * momentum_ref[...] + total * inv_width
        ).astype(jnp.bfloat16)

    return pl.pallas_call(
        body,
        grid=(size // step,),
        in_specs=[
            pl.BlockSpec((tokens, step), lambda i: (0, first_column + i)),
            pl.BlockSpec((tokens, depth), lambda i: (0, 0)),
            pl.BlockSpec((step, depth), lambda i: (first + i, 0)),
        ]
        + [pl.BlockSpec(memory_space=pl.ANY)] * len(gates),
        out_specs=pl.BlockSpec((step, depth), lambda i: (i, 0)),
        out_shape=jax.ShapeDtypeStruct((size, depth), jnp.bfloat16),
        compiler_params=params_of(24 * MIB),
        cost_estimate=cost_of(
            tokens * size * depth, 6 * size * depth + 2 * tokens * depth
        ),
        name="moment_rows",
    )(attended, grads, momentum, *gates)


def averaged_rows(
    rate, params, far_params, far_start, moment, far_moment, start, size, results
):
    depth = params.shape[1]
    step = math.gcd(size, 32)
    first = start // step
    far_first = (start - far_start) // step

    def body(rate_ref, params_ref, far_params_ref, moment_ref, far_moment_ref, *refs):
        new_params_ref, new_momentum_ref = refs[-2:]
        mean_moment = 0.5 * (
            moment_ref[...].astype(jnp.float32) + far_moment_ref[...].astype(jnp.float32)
        )
        mean_params = 0.5 * (params_ref[...] + far_params_ref[...].astype(jnp.float32))
        new_momentum_ref[...] = mean_moment
        new_params_ref[...] = mean_params - rate_ref[0] * mean_moment

    whole_spec = pl.BlockSpec((step, depth), lambda i: (first + i, 0))
    part_spec = pl.BlockSpec((step, depth), lambda i: (i, 0))
    kept = [] if results is None else list(results)
    return pl.pallas_call(
        body,
        grid=(size // step,),
        in_specs=[
            pl.BlockSpec(memory_space=pltpu.SMEM),
            whole_spec,
            pl.BlockSpec((step, depth), lambda i: (far_first + i, 0)),
            part_spec,
            part_spec,
        ]
        + [pl.BlockSpec(memory_space=pl.ANY)] * len(kept),
        out_specs=[whole_spec] * 2,
        out_shape=[pltpu.HBM(params.shape, jnp.float32)] * 2,
        input_output_aliases={5 + i: i for i in range(len(kept))},
        compiler_params=params_of(8 * MIB),
        cost_estimate=cost_of(3 * size * depth, 18 * size * depth),
        name="averaged_rows",
    )(rate, params, far_params, moment, far_moment, *kept)


def placed_heads(place, pack, results, shift, count, group, groups):
    rows, width = results[0].shape
    span = width // count // groups

    def body(place_ref, pack_ref, *refs):
        for part in range(3):
            refs[3 + part][...] = pack_ref[part]

    spec = pl.BlockSpec(
        (rows, span),
        lambda i, place_ref: (0, lax.rem(place_ref[0] + shift, count) * groups + group),
    )
    return pl.pallas_call(
        body,
        grid_spec=pltpu.PrefetchScalarGridSpec(
            num_scalar_prefetch=1,
            grid=(1,),
            in_specs=[pl.BlockSpec((3, rows, span), lambda i, place_ref: (0, 0, 0))]
            + [pl.BlockSpec(memory_space=pl.ANY)] * 3,
            out_specs=[spec] * 3,
        ),
        out_shape=[pltpu.HBM((rows, width), jnp.bfloat16)] * 3,
        input_output_aliases={2 + part: part for part in range(3)},
        compiler_params=params_of(8 * MIB),
        cost_estimate=cost_of(0, 12 * rows * span),
        name="placed_heads",
    )(place, pack, *results)


def score_bias(me, count, own_ids, far_ids, block_mask):
    rows = own_ids.shape[0]
    blocks = block_mask.shape[0]
    block_rows = rows * count // blocks
    stems = jnp.concatenate([own_ids] + far_ids) // CODES
    position = jnp.concatenate(
        [lax.rem(me + count - s, count) * rows + jnp.arange(rows) for s in range(count)]
    )
    block_of = position // block_rows
    picks = (block_of[:, None] == jnp.arange(blocks)[None, :]).astype(jnp.float32)
    spread = jnp.dot(jnp.dot(picks, block_mask.astype(jnp.float32)), picks.T)
    allowed = (
        (spread > 0.5)
        & (position[None, :] <= position[:, None])
        & ((stems[:, None] == stems[None, :]) | (block_of[:, None] == block_of[None, :]))
    )
    return jnp.where(allowed, 0.0, -1e30)


def step_with_partner(
    bit_level,
    query_rows,
    key_rows,
    value_rows,
    out_grad,
    params,
    momentum,
    token_ids,
    block_mask,
    rate,
):
    count = lax.axis_size("fsdp")
    me = lax.axis_index("fsdp")
    place = me.astype(jnp.int32).reshape(1)
    local, inner = params.shape[0], params.shape[0] * count
    route = partner_route(lax.axis_size("dp"), bit_level)
    shifts = range(1, count)
    near = bit_level == 0
    groups = math.gcd(local // HD, 2) if near else 1
    span = local // groups
    if near:
        chunks = [[(group * span, span)] for group in range(groups)]
    else:
        chunks = [row_chunks(group * span, span) for group in range(groups)]
        params = in_hbm(params)

    tensors = (query_rows, key_rows, value_rows)
    rings = [shift_route(count, shift) for shift in shifts]
    far_params = []
    if not near:
        cut = chunks[0][-2][0] if len(chunks[0]) > 2 else local
        for start, size in ((0, cut), (cut, local - cut)):
            if size:
                short = short_rows(params, start, size)
                far_params.append((start, size, lax.ppermute(short, "dp", route)))

    packs, ids_sent = [], token_ids
    for group in range(groups):
        packs.append([])
        for shift, ring in zip(shifts, rings):
            pack, ids_copy = packed_heads(
                place, tensors, out_grad, token_ids, shift, count, group, groups
            )
            packs[group].append(lax.ppermute(pack, "fsdp", ring))
            if not near:
                ids_sent = ids_copy
    far_ids = [lax.ppermute(ids_sent, "fsdp", ring) for ring in rings]

    bias = score_bias(me, count, token_ids, far_ids, block_mask)
    attended, returned, results, grads = [], [], None, out_grad
    for group in range(groups):
        outs = attention_step(
            place,
            bias,
            tensors,
            packs[group],
            grads,
            params,
            results,
            count,
            group,
            groups,
            near,
        )
        attended.append(outs[0])
        results, backs = outs[1:4], outs[4 : 4 + len(shifts)]
        if group == 0:
            grads = outs[4 + len(shifts)]
        if near:
            far = lax.ppermute(outs[-1], "dp", route)
            far_params.append((group * span, span, far))
        returned.append(
            [
                lax.ppermute(back, "fsdp", shift_route(count, -shift))
                for shift, back in zip(shifts, backs)
            ]
        )
    sent = []
    for group in range(groups):
        gates = returned[0][:1] if group else []
        for start, size in chunks[group]:
            moment = moment_rows(
                attended[group], grads, momentum, start, size, group * span, inner, gates
            )
            sent.append((start, size, moment, lax.ppermute(moment, "dp", route)))
    means = None
    for start, size, moment, far_moment in sent:
        far_start, far = next(
            (first, rows) for first, many, rows in far_params if first <= start < first + many
        )
        means = averaged_rows(
            rate, params, far, far_start, moment, far_moment, start, size, means
        )
    for group in range(groups):
        for shift, pack in zip(shifts, returned[group]):
            results = placed_heads(place, pack, results, shift, count, group, groups)
    return (*results, *means)


def shards(
    query_rows, key_rows, value_rows, out_grad, params, momentum, token_ids, block_mask, step_index
):
    step_value = step_index[0]
    correction = 1.0 / (
        1.0 - jnp.exp((step_value + 1).astype(jnp.float32) * math.log(MOMENTUM_RATE))
    )
    rate = (LEARN_RATE * correction).reshape(1)
    return lax.switch(
        step_value % 4,
        [functools.partial(step_with_partner, bit_level) for bit_level in range(4)],
        query_rows,
        key_rows,
        value_rows,
        out_grad,
        params,
        momentum,
        token_ids,
        block_mask,
        rate,
    )


def solution(mesh):
    rows = P(("dp", "fsdp"), None)
    return jax.shard_map(
        shards,
        mesh=mesh,
        in_specs=(rows,) * 6 + (P(("dp", "fsdp")), P(), P()),
        out_specs=(rows,) * 5,
        check_vma=False,
    )
```

```python
import functools
import math

import jax
import jax.numpy as jnp
from jax import lax
from jax.experimental import pallas as pl
from jax.experimental.pallas import tpu as pltpu
from jax.sharding import PartitionSpec as P

HD = 128
CODES = 2048
MOMENTUM_RATE = 0.9
LEARN_RATE = 0.25
MIB = 1 << 20

CONTRACT_LAST = (((1,), (1,)), ((), ()))
CONTRACT_FIRST = (((0,), (0,)), ((), ()))


def dot_f32(left, right, dims):
    return lax.dot_general(left, right, dims, preferred_element_type=jnp.float32)


def cost_of(macs, moved):
    return pl.CostEstimate(flops=2 * macs, bytes_accessed=moved, transcendentals=0)


def params_of(limit):
    return pltpu.CompilerParams(vmem_limit_bytes=limit)


def row_chunks(start, rows):
    chunks, end = [], start + rows
    while start < end:
        left = (end - start) // HD
        size = HD * (left // 2 if left > 2 else 1)
        chunks.append((start, size))
        start += size
    return chunks


def in_hbm(array):
    return pltpu.with_memory_space_constraint(array, pltpu.HBM)


def partner_route(count, bit_level):
    route = []
    for low in range(count):
        high = low | 1 << bit_level
        if high != low and high < count:
            route += [(low, high), (high, low)]
    return route


def shift_route(count, shift):
    return [(source, (source + shift) % count) for source in range(count)]


def short_rows(params, start, size):
    width = params.shape[1]
    step = math.gcd(size, 2 * HD)

    def body(wide_ref, short_ref):
        short_ref[...] = wide_ref[...].astype(jnp.bfloat16)

    return pl.pallas_call(
        body,
        grid=(size // step,),
        in_specs=[pl.BlockSpec((step, width), lambda i: (start // step + i, 0))],
        out_specs=pl.BlockSpec((step, width), lambda i: (i, 0)),
        out_shape=jax.ShapeDtypeStruct((size, width), jnp.bfloat16),
        compiler_params=params_of(12 * MIB),
        cost_estimate=cost_of(0, 6 * size * width),
        name="short_rows",
    )(params)


def packed_heads(place, tensors, out_grad, token_ids, shift, count, group, groups):
    rows, width = tensors[0].shape
    span = width // count // groups
    slabs = out_grad.shape[1] // span if group == 0 else 0

    def body(place_ref, query_ref, key_ref, value_ref, *refs):
        pack_ref = refs[-2] if slabs else refs[-1]
        for slab in range(slabs):
            pack_ref[slab] = refs[0][:, slab * span : (slab + 1) * span]
        if slabs:
            refs[-1][...] = refs[1][...]
        pack_ref[slabs] = query_ref[...]
        pack_ref[slabs + 1] = key_ref[...]
        pack_ref[slabs + 2] = value_ref[...]

    spec = pl.BlockSpec(
        (rows, span),
        lambda i, place_ref: (0, lax.rem(place_ref[0] + shift, count) * groups + group),
    )
    grad_spec = pl.BlockSpec(out_grad.shape, lambda i, place_ref: (0, 0))
    ids_spec = pl.BlockSpec((1, rows), lambda i, place_ref: (0, 0))
    outs = pl.pallas_call(
        body,
        grid_spec=pltpu.PrefetchScalarGridSpec(
            num_scalar_prefetch=1,
            grid=(1,),
            in_specs=[spec] * 3
            + [grad_spec, ids_spec] * (slabs > 0),
            out_specs=[
                pl.BlockSpec((slabs + 3, rows, span), lambda i, place_ref: (0, 0, 0))
            ]
            + [ids_spec] * (slabs > 0),
        ),
        out_shape=[jax.ShapeDtypeStruct((slabs + 3, rows, span), out_grad.dtype)]
        + [jax.ShapeDtypeStruct((1, rows), token_ids.dtype)] * (slabs > 0),
        compiler_params=params_of(12 * MIB),
        cost_estimate=cost_of(0, 4 * (slabs + 3) * rows * span),
        name="packed_heads",
    )(place, *tensors, *[out_grad, token_ids.reshape(1, rows)] * (slabs > 0))
    return outs[0], outs[1].reshape(rows) if slabs else None


def attention_step(
    place, bias, tensors, packs, grads, params, results, count, group, groups, short_out
):
    rows, width = tensors[0].shape
    tokens = rows * count
    heads = width // count // HD // groups
    together = math.gcd(heads, 2)
    span = together * HD
    steps = heads // together
    depth = params.shape[1]
    first = group == 0
    slabs = packs[0].shape[0] - 3 if packs else 0
    slab = heads * HD
    kept = [] if results is None else list(results)
    score_scale = 1.0 / math.sqrt(HD)
    inv_width = 1.0 / math.sqrt(width)
    far = count - 1

    def body(place_ref, bias_ref, query_ref, key_ref, value_ref, *refs):
        pack_refs, refs = [refs[3 * s : 3 * s + 3] for s in range(far)], refs[3 * far :]
        slab_refs, refs = refs[: far * first], refs[far * first :]
        grads_ref, params_ref = refs[:2]
        refs = refs[2 + len(kept) :]
        attended_ref, dq_ref, dk_ref, dv_ref = refs[:4]
        back_refs = refs[4 : 4 + far]

        if first:
            own_ref, grads_ref = grads_ref, refs[4 + far]

            @pl.when(pl.program_id(0) == 0)
            def _():
                grads_ref[:rows, :] = own_ref[...]
                for s in range(far):
                    for at in range(slabs):
                        grads_ref[
                            (s + 1) * rows : (s + 2) * rows, at * slab : (at + 1) * slab
                        ] = slab_refs[s][at]

        weight = params_ref[...].astype(jnp.bfloat16)
        if short_out:
            refs[-1][...] = weight
        grad_heads = (dot_f32(grads_ref[...], weight, CONTRACT_LAST) * inv_width).astype(
            jnp.bfloat16
        )
        for g in range(together):
            cols = slice(g * HD, (g + 1) * HD)

            def whole(own_ref, part):
                return jnp.concatenate(
                    [own_ref[:, cols]] + [far_refs[part][:, cols] for far_refs in pack_refs],
                    axis=0,
                )

            query, key, value = whole(query_ref, 0), whole(key_ref, 1), whole(value_ref, 2)
            grad = grad_heads[:, cols]
            scores = dot_f32(query, key, CONTRACT_LAST) * score_scale + bias_ref[...]
            top = jnp.max(scores, axis=-1, keepdims=True)
            terms = jnp.exp(scores - top)
            prob = terms * (1.0 / jnp.sum(terms, axis=-1, keepdims=True))
            prob16 = prob.astype(jnp.bfloat16)
            attended_ref[:, cols] = jnp.dot(
                prob16, value, preferred_element_type=jnp.float32
            ).astype(jnp.bfloat16)
            grad_value = dot_f32(prob16, grad, CONTRACT_FIRST).astype(jnp.bfloat16)
            grad_prob = dot_f32(grad, value, CONTRACT_LAST)
            row_dot = jnp.sum(prob * grad_prob, axis=-1, keepdims=True)
            grad_score = (prob * (grad_prob - row_dot) * score_scale).astype(jnp.bfloat16)
            grad_query = jnp.dot(
                grad_score, key, preferred_element_type=jnp.float32
            ).astype(jnp.bfloat16)
            grad_key = dot_f32(grad_score, query, CONTRACT_FIRST).astype(jnp.bfloat16)
            for part, (out_ref, result) in enumerate(
                ((dq_ref, grad_query), (dk_ref, grad_key), (dv_ref, grad_value))
            ):
                out_ref[:, cols] = result[:rows]
                for s in range(far):
                    back_refs[s][part, :, cols] = result[(s + 1) * rows : (s + 2) * rows]

    own_spec = pl.BlockSpec(
        (rows, span), lambda i, place_ref: (0, (place_ref[0] * groups + group) * steps + i)
    )
    pack_specs = [
        pl.BlockSpec((None, rows, span), lambda i, place_ref, part=part: (part, 0, i))
        for part in range(slabs, slabs + 3)
    ]
    back_spec = pl.BlockSpec((3, rows, span), lambda i, place_ref: (0, 0, i))
    all_spec = pl.BlockSpec((tokens, depth), lambda i, place_ref: (0, 0))
    own_shape = pltpu.HBM((rows, width), jnp.bfloat16)
    macs = tokens * depth * heads * HD + 5 * heads * tokens * tokens * HD
    operands = [place, bias, *tensors]
    for pack in packs:
        operands += [pack] * 3
    in_specs = (
        [pl.BlockSpec((tokens, tokens), lambda i, place_ref: (0, 0))]
        + [own_spec] * 3
        + pack_specs * far
    )
    if first:
        operands += packs
        in_specs += [
            pl.BlockSpec((slabs, rows, slab), lambda i, place_ref: (0, 0, 0))
        ] * far + [pl.BlockSpec((rows, depth), lambda i, place_ref: (0, 0))]
    else:
        in_specs += [all_spec]
    operands += [grads, params]
    in_specs += [pl.BlockSpec((span, depth), lambda i, place_ref: (group * steps + i, 0))]
    aliases = {len(operands) + i: 1 + i for i in range(len(kept))}
    in_specs += [pl.BlockSpec(memory_space=pl.ANY)] * len(kept)
    return pl.pallas_call(
        body,
        grid_spec=pltpu.PrefetchScalarGridSpec(
            num_scalar_prefetch=1,
            grid=(steps,),
            in_specs=in_specs,
            out_specs=[pl.BlockSpec((tokens, span), lambda i, place_ref: (0, i))]
            + [own_spec] * 3
            + [back_spec] * far
            + [all_spec] * first
            + [pl.BlockSpec((span, depth), lambda i, place_ref: (i, 0))] * short_out,
        ),
        out_shape=[jax.ShapeDtypeStruct((tokens, heads * HD), jnp.bfloat16)]
        + [own_shape] * 3
        + [jax.ShapeDtypeStruct((3, rows, heads * HD), jnp.bfloat16)] * far
        + [jax.ShapeDtypeStruct((tokens, depth), jnp.bfloat16)] * first
        + [jax.ShapeDtypeStruct((heads * HD, depth), jnp.bfloat16)] * short_out,
        input_output_aliases=aliases,
        compiler_params=params_of((24 if tokens <= 256 else 56) * MIB),
        cost_estimate=cost_of(macs, heads * HD * (4 * depth + 16 * tokens)),
        name="attention_step",
    )(*operands, *kept)


def moment_rows(attended, grads, momentum, start, size, group_start, inner, gates):
    tokens, depth = grads.shape
    step = math.gcd(size, 2 * HD)
    first = start // step
    first_column = (start - group_start) // step
    inv_width = 1.0 / math.sqrt(inner)


    def body(attended_ref, grads_ref, momentum_ref, *refs):
        total = dot_f32(attended_ref[...], grads_ref[...], CONTRACT_FIRST)
        refs[-1][...] = (
            MOMENTUM_RATE * momentum_ref[...] + total * inv_width
        ).astype(jnp.bfloat16)

    return pl.pallas_call(
        body,
        grid=(size // step,),
        in_specs=[
            pl.BlockSpec((tokens, step), lambda i: (0, first_column + i)),
            pl.BlockSpec((tokens, depth), lambda i: (0, 0)),
            pl.BlockSpec((step, depth), lambda i: (first + i, 0)),
        ]
        + [pl.BlockSpec(memory_space=pl.ANY)] * len(gates),
        out_specs=pl.BlockSpec((step, depth), lambda i: (i, 0)),
        out_shape=jax.ShapeDtypeStruct((size, depth), jnp.bfloat16),
        compiler_params=params_of(24 * MIB),
        cost_estimate=cost_of(
            tokens * size * depth, 6 * size * depth + 2 * tokens * depth
        ),
        name="moment_rows",
    )(attended, grads, momentum, *gates)


def averaged_rows(
    rate, params, far_params, far_start, moment, far_moment, start, size, results
):
    depth = params.shape[1]
    step = math.gcd(size, HD if size > HD else HD // 2)
    first = start // step
    far_first = (start - far_start) // step

    def body(rate_ref, params_ref, far_params_ref, moment_ref, far_moment_ref, *refs):
        new_params_ref, new_momentum_ref = refs[-2:]
        mean_moment = 0.5 * (
            moment_ref[...].astype(jnp.float32) + far_moment_ref[...].astype(jnp.float32)
        )
        mean_params = 0.5 * (params_ref[...] + far_params_ref[...].astype(jnp.float32))
        new_momentum_ref[...] = mean_moment
        new_params_ref[...] = mean_params - rate_ref[0] * mean_moment

    whole_spec = pl.BlockSpec((step, depth), lambda i: (first + i, 0))
    part_spec = pl.BlockSpec((step, depth), lambda i: (i, 0))
    kept = [] if results is None else list(results)
    return pl.pallas_call(
        body,
        grid=(size // step,),
        in_specs=[
            pl.BlockSpec(memory_space=pltpu.SMEM),
            whole_spec,
            pl.BlockSpec((step, depth), lambda i: (far_first + i, 0)),
            part_spec,
            part_spec,
        ]
        + [pl.BlockSpec(memory_space=pl.ANY)] * len(kept),
        out_specs=[whole_spec] * 2,
        out_shape=[pltpu.HBM(params.shape, jnp.float32)] * 2,
        input_output_aliases={5 + i: i for i in range(len(kept))},
        compiler_params=params_of(16 * MIB),
        cost_estimate=cost_of(3 * size * depth, 18 * size * depth),
        name="averaged_rows",
    )(rate, params, far_params, moment, far_moment, *kept)


def placed_heads(place, pack, results, shift, count, group, groups):
    rows, width = results[0].shape
    span = width // count // groups

    def body(place_ref, pack_ref, *refs):
        for part in range(3):
            refs[3 + part][...] = pack_ref[part]

    spec = pl.BlockSpec(
        (rows, span),
        lambda i, place_ref: (0, lax.rem(place_ref[0] + shift, count) * groups + group),
    )
    return pl.pallas_call(
        body,
        grid_spec=pltpu.PrefetchScalarGridSpec(
            num_scalar_prefetch=1,
            grid=(1,),
            in_specs=[pl.BlockSpec((3, rows, span), lambda i, place_ref: (0, 0, 0))]
            + [pl.BlockSpec(memory_space=pl.ANY)] * 3,
            out_specs=[spec] * 3,
        ),
        out_shape=[pltpu.HBM((rows, width), jnp.bfloat16)] * 3,
        input_output_aliases={2 + part: part for part in range(3)},
        compiler_params=params_of(8 * MIB),
        cost_estimate=cost_of(0, 12 * rows * span),
        name="placed_heads",
    )(place, pack, *results)


def score_bias(me, count, own_ids, far_ids, block_mask):
    rows = own_ids.shape[0]
    blocks = block_mask.shape[0]
    block_rows = rows * count // blocks
    stems = jnp.concatenate([own_ids] + far_ids) // CODES
    position = jnp.concatenate(
        [lax.rem(me + count - s, count) * rows + jnp.arange(rows) for s in range(count)]
    )
    block_of = position // block_rows
    picks = (block_of[:, None] == jnp.arange(blocks)[None, :]).astype(jnp.float32)
    spread = jnp.dot(jnp.dot(picks, block_mask.astype(jnp.float32)), picks.T)
    allowed = (
        (spread > 0.5)
        & (position[None, :] <= position[:, None])
        & ((stems[:, None] == stems[None, :]) | (block_of[:, None] == block_of[None, :]))
    )
    return jnp.where(allowed, 0.0, -1e30)


def step_with_partner(
    bit_level,
    query_rows,
    key_rows,
    value_rows,
    out_grad,
    params,
    momentum,
    token_ids,
    block_mask,
    rate,
):
    count = lax.axis_size("fsdp")
    me = lax.axis_index("fsdp")
    place = me.astype(jnp.int32).reshape(1)
    local, inner = params.shape[0], params.shape[0] * count
    route = partner_route(lax.axis_size("dp"), bit_level)
    shifts = range(1, count)
    near = bit_level == 0
    groups = math.gcd(local // HD, 2) if near else 1
    span = local // groups
    if near:
        chunks = [[(group * span, span)] for group in range(groups)]
    else:
        chunks = [row_chunks(group * span, span) for group in range(groups)]

    tensors = (query_rows, key_rows, value_rows)
    rings = [shift_route(count, shift) for shift in shifts]
    far_params = []
    if not near:
        params = in_hbm(params)
        cut = chunks[0][-2][0] if len(chunks[0]) > 2 else local
        for start, size in ((0, cut), (cut, local - cut)):
            if size:
                short = short_rows(params, start, size)
                far_params.append((start, size, lax.ppermute(short, "dp", route)))

    packs, ids_sent = [], token_ids
    for group in range(groups):
        packs.append([])
        for shift, ring in zip(shifts, rings):
            pack, ids_copy = packed_heads(
                place, tensors, out_grad, token_ids, shift, count, group, groups
            )
            packs[group].append(lax.ppermute(pack, "fsdp", ring))
            if not near:
                ids_sent = ids_copy
    far_ids = [lax.ppermute(ids_sent, "fsdp", ring) for ring in rings]

    bias = score_bias(me, count, token_ids, far_ids, block_mask)
    attended, returned, results, grads = [], [], None, out_grad
    for group in range(groups):
        outs = attention_step(
            place,
            bias,
            tensors,
            packs[group],
            grads,
            params,
            results,
            count,
            group,
            groups,
            near,
        )
        attended.append(outs[0])
        results, backs = outs[1:4], outs[4 : 4 + len(shifts)]
        if group == 0:
            grads = outs[4 + len(shifts)]
        if near:
            far = lax.ppermute(outs[-1], "dp", route)
            far_params.append((group * span, span, far))
        returned.append(
            [
                lax.ppermute(back, "fsdp", shift_route(count, -shift))
                for shift, back in zip(shifts, backs)
            ]
        )
    sent = []
    for group in range(groups):
        gates = returned[0][:1] if group else []
        for start, size in chunks[group]:
            moment = moment_rows(
                attended[group], grads, momentum, start, size, group * span, inner, gates
            )
            sent.append((start, size, moment, lax.ppermute(moment, "dp", route)))
    means = None
    for start, size, moment, far_moment in sent:
        far_start, far = next(
            (first, rows) for first, many, rows in far_params if first <= start < first + many
        )
        means = averaged_rows(
            rate,
            params,
            far,
            far_start,
            moment,
            far_moment,
            start,
            size,
            means,
        )
    for group in range(groups):
        for shift, pack in zip(shifts, returned[group]):
            results = placed_heads(place, pack, results, shift, count, group, groups)
    return (*results, *means)


def shards(
    query_rows, key_rows, value_rows, out_grad, params, momentum, token_ids, block_mask, step_index
):
    step_value = step_index[0]
    correction = 1.0 / (
        1.0 - jnp.exp((step_value + 1).astype(jnp.float32) * math.log(MOMENTUM_RATE))
    )
    rate = (LEARN_RATE * correction).reshape(1)
    return lax.switch(
        step_value % 4,
        [functools.partial(step_with_partner, bit_level) for bit_level in range(4)],
        query_rows,
        key_rows,
        value_rows,
        out_grad,
        params,
        momentum,
        token_ids,
        block_mask,
        rate,
    )


def solution(mesh):
    rows = P(("dp", "fsdp"), None)
    return jax.shard_map(
        shards,
        mesh=mesh,
        in_specs=(rows,) * 6 + (P(("dp", "fsdp")), P(), P()),
        out_specs=(rows,) * 5,
        check_vma=False,
    )
```

```python
import functools
import math

import jax
import jax.numpy as jnp
from jax import lax
from jax.experimental import pallas as pl
from jax.experimental.pallas import tpu as pltpu
from jax.sharding import PartitionSpec as P

HD = 128
CODES = 2048
MOMENTUM_RATE = 0.9
LEARN_RATE = 0.25
MIB = 1 << 20

CONTRACT_LAST = (((1,), (1,)), ((), ()))
CONTRACT_FIRST = (((0,), (0,)), ((), ()))


def dot_f32(left, right, dims):
    return lax.dot_general(left, right, dims, preferred_element_type=jnp.float32)


def cost_of(macs, moved):
    return pl.CostEstimate(flops=2 * macs, bytes_accessed=moved, transcendentals=0)


def params_of(limit):
    return pltpu.CompilerParams(vmem_limit_bytes=limit)


def row_chunks(start, rows):
    chunks, end = [], start + rows
    while start < end:
        left = (end - start) // HD
        size = HD * (left // 2 if left > 2 else 1)
        chunks.append((start, size))
        start += size
    return chunks


def in_hbm(array):
    return pltpu.with_memory_space_constraint(array, pltpu.HBM)


def partner_route(count, bit_level):
    route = []
    for low in range(count):
        high = low | 1 << bit_level
        if high != low and high < count:
            route += [(low, high), (high, low)]
    return route


def shift_route(count, shift):
    return [(source, (source + shift) % count) for source in range(count)]


def short_rows(params, start, size):
    width = params.shape[1]
    piece = math.gcd(size, HD)
    pieces = size // piece

    def body(wide_ref, short_ref, wide, short, in_sem, out_sem):
        reads = [
            pltpu.make_async_copy(
                wide_ref.at[pl.ds(start + i * piece, piece)], wide.at[i], in_sem.at[i]
            )
            for i in range(pieces)
        ]
        writes = [
            pltpu.make_async_copy(
                short.at[i], short_ref.at[pl.ds(i * piece, piece)], out_sem.at[i]
            )
            for i in range(pieces)
        ]
        for read in reads:
            read.start()
        for i in range(pieces):
            reads[i].wait()
            short[i] = wide[i].astype(jnp.bfloat16)
            writes[i].start()
        for write in writes:
            write.wait()

    return pl.pallas_call(
        body,
        in_specs=[pl.BlockSpec(memory_space=pl.ANY)],
        out_specs=pl.BlockSpec(memory_space=pl.ANY),
        out_shape=jax.ShapeDtypeStruct((size, width), jnp.bfloat16),
        scratch_shapes=[
            pltpu.VMEM((pieces, piece, width), jnp.float32),
            pltpu.VMEM((pieces, piece, width), jnp.bfloat16),
            pltpu.SemaphoreType.DMA((pieces,)),
            pltpu.SemaphoreType.DMA((pieces,)),
        ],
        compiler_params=params_of(6 * size * width + 2 * MIB),
        cost_estimate=cost_of(0, 6 * size * width),
        name="short_rows",
    )(params)


def packed_heads(place, tensors, out_grad, token_ids, shift, count, group, groups):
    rows, width = tensors[0].shape
    span = width // count // groups
    slabs = out_grad.shape[1] // span if group == 0 else 0

    def body(place_ref, query_ref, key_ref, value_ref, *refs):
        pack_ref = refs[-2] if slabs else refs[-1]
        for slab in range(slabs):
            pack_ref[slab] = refs[0][:, slab * span : (slab + 1) * span]
        if slabs:
            refs[-1][...] = refs[1][...]
        pack_ref[slabs] = query_ref[...]
        pack_ref[slabs + 1] = key_ref[...]
        pack_ref[slabs + 2] = value_ref[...]

    spec = pl.BlockSpec(
        (rows, span),
        lambda i, place_ref: (0, lax.rem(place_ref[0] + shift, count) * groups + group),
    )
    grad_spec = pl.BlockSpec(out_grad.shape, lambda i, place_ref: (0, 0))
    ids_spec = pl.BlockSpec((1, rows), lambda i, place_ref: (0, 0))
    outs = pl.pallas_call(
        body,
        grid_spec=pltpu.PrefetchScalarGridSpec(
            num_scalar_prefetch=1,
            grid=(1,),
            in_specs=[spec] * 3
            + [grad_spec, ids_spec] * (slabs > 0),
            out_specs=[
                pl.BlockSpec((slabs + 3, rows, span), lambda i, place_ref: (0, 0, 0))
            ]
            + [ids_spec] * (slabs > 0),
        ),
        out_shape=[jax.ShapeDtypeStruct((slabs + 3, rows, span), out_grad.dtype)]
        + [jax.ShapeDtypeStruct((1, rows), token_ids.dtype)] * (slabs > 0),
        compiler_params=params_of(12 * MIB),
        cost_estimate=cost_of(0, 4 * (slabs + 3) * rows * span),
        name="packed_heads",
    )(place, *tensors, *[out_grad, token_ids.reshape(1, rows)] * (slabs > 0))
    return outs[0], outs[1].reshape(rows) if slabs else None


def attention_step(
    place, bias, tensors, packs, grads, params, results, count, group, groups, short_out
):
    rows, width = tensors[0].shape
    tokens = rows * count
    heads = width // count // HD // groups
    together = math.gcd(heads, 2)
    span = together * HD
    steps = heads // together
    depth = params.shape[1]
    first = group == 0
    slabs = packs[0].shape[0] - 3 if packs else 0
    slab = heads * HD
    kept = [] if results is None else list(results)
    score_scale = 1.0 / math.sqrt(HD)
    inv_width = 1.0 / math.sqrt(width)
    far = count - 1

    def body(place_ref, bias_ref, query_ref, key_ref, value_ref, *refs):
        pack_refs, refs = [refs[3 * s : 3 * s + 3] for s in range(far)], refs[3 * far :]
        slab_refs, refs = refs[: far * first], refs[far * first :]
        grads_ref, params_ref = refs[:2]
        refs = refs[2 + len(kept) :]
        attended_ref, dq_ref, dk_ref, dv_ref = refs[:4]
        back_refs = refs[4 : 4 + far]

        if first:
            own_ref, grads_ref = grads_ref, refs[4 + far]

            @pl.when(pl.program_id(0) == 0)
            def _():
                grads_ref[:rows, :] = own_ref[...]
                for s in range(far):
                    for at in range(slabs):
                        grads_ref[
                            (s + 1) * rows : (s + 2) * rows, at * slab : (at + 1) * slab
                        ] = slab_refs[s][at]

        weight = params_ref[...].astype(jnp.bfloat16)
        if short_out:
            refs[-1][...] = weight
        grad_heads = (dot_f32(grads_ref[...], weight, CONTRACT_LAST) * inv_width).astype(
            jnp.bfloat16
        )
        for g in range(together):
            cols = slice(g * HD, (g + 1) * HD)

            def whole(own_ref, part):
                return jnp.concatenate(
                    [own_ref[:, cols]] + [far_refs[part][:, cols] for far_refs in pack_refs],
                    axis=0,
                )

            query, key, value = whole(query_ref, 0), whole(key_ref, 1), whole(value_ref, 2)
            grad = grad_heads[:, cols]
            scores = dot_f32(query, key, CONTRACT_LAST) * score_scale + bias_ref[...]
            top = jnp.max(scores, axis=-1, keepdims=True)
            terms = jnp.exp(scores - top)
            prob = terms * (1.0 / jnp.sum(terms, axis=-1, keepdims=True))
            prob16 = prob.astype(jnp.bfloat16)
            attended_ref[:, cols] = jnp.dot(
                prob16, value, preferred_element_type=jnp.float32
            ).astype(jnp.bfloat16)
            grad_value = dot_f32(prob16, grad, CONTRACT_FIRST).astype(jnp.bfloat16)
            grad_prob = dot_f32(grad, value, CONTRACT_LAST)
            row_dot = jnp.sum(prob * grad_prob, axis=-1, keepdims=True)
            grad_score = (prob * (grad_prob - row_dot) * score_scale).astype(jnp.bfloat16)
            grad_query = jnp.dot(
                grad_score, key, preferred_element_type=jnp.float32
            ).astype(jnp.bfloat16)
            grad_key = dot_f32(grad_score, query, CONTRACT_FIRST).astype(jnp.bfloat16)
            for part, (out_ref, result) in enumerate(
                ((dq_ref, grad_query), (dk_ref, grad_key), (dv_ref, grad_value))
            ):
                out_ref[:, cols] = result[:rows]
                for s in range(far):
                    back_refs[s][part, :, cols] = result[(s + 1) * rows : (s + 2) * rows]

    own_spec = pl.BlockSpec(
        (rows, span), lambda i, place_ref: (0, (place_ref[0] * groups + group) * steps + i)
    )
    pack_specs = [
        pl.BlockSpec((None, rows, span), lambda i, place_ref, part=part: (part, 0, i))
        for part in range(slabs, slabs + 3)
    ]
    back_spec = pl.BlockSpec((3, rows, span), lambda i, place_ref: (0, 0, i))
    all_spec = pl.BlockSpec((tokens, depth), lambda i, place_ref: (0, 0))
    own_shape = pltpu.HBM((rows, width), jnp.bfloat16)
    macs = tokens * depth * heads * HD + 5 * heads * tokens * tokens * HD
    operands = [place, bias, *tensors]
    for pack in packs:
        operands += [pack] * 3
    in_specs = (
        [pl.BlockSpec((tokens, tokens), lambda i, place_ref: (0, 0))]
        + [own_spec] * 3
        + pack_specs * far
    )
    if first:
        operands += packs
        in_specs += [
            pl.BlockSpec((slabs, rows, slab), lambda i, place_ref: (0, 0, 0))
        ] * far + [pl.BlockSpec((rows, depth), lambda i, place_ref: (0, 0))]
    else:
        in_specs += [all_spec]
    operands += [grads, params]
    in_specs += [pl.BlockSpec((span, depth), lambda i, place_ref: (group * steps + i, 0))]
    aliases = {len(operands) + i: 1 + i for i in range(len(kept))}
    in_specs += [pl.BlockSpec(memory_space=pl.ANY)] * len(kept)
    return pl.pallas_call(
        body,
        grid_spec=pltpu.PrefetchScalarGridSpec(
            num_scalar_prefetch=1,
            grid=(steps,),
            in_specs=in_specs,
            out_specs=[pl.BlockSpec((tokens, span), lambda i, place_ref: (0, i))]
            + [own_spec] * 3
            + [back_spec] * far
            + [all_spec] * first
            + [pl.BlockSpec((span, depth), lambda i, place_ref: (i, 0))] * short_out,
        ),
        out_shape=[jax.ShapeDtypeStruct((tokens, heads * HD), jnp.bfloat16)]
        + [own_shape] * 3
        + [jax.ShapeDtypeStruct((3, rows, heads * HD), jnp.bfloat16)] * far
        + [jax.ShapeDtypeStruct((tokens, depth), jnp.bfloat16)] * first
        + [jax.ShapeDtypeStruct((heads * HD, depth), jnp.bfloat16)] * short_out,
        input_output_aliases=aliases,
        compiler_params=params_of((24 if tokens <= 256 else 56) * MIB),
        cost_estimate=cost_of(macs, heads * HD * (4 * depth + 16 * tokens)),
        name="attention_step",
    )(*operands, *kept)


def moment_rows(attended, grads, momentum, start, size, group_start, inner, gates):
    tokens, depth = grads.shape
    step = math.gcd(size, 2 * HD)
    first = start // step
    first_column = (start - group_start) // step
    inv_width = 1.0 / math.sqrt(inner)


    def body(attended_ref, grads_ref, momentum_ref, *refs):
        total = dot_f32(attended_ref[...], grads_ref[...], CONTRACT_FIRST)
        refs[-1][...] = (
            MOMENTUM_RATE * momentum_ref[...] + total * inv_width
        ).astype(jnp.bfloat16)

    return pl.pallas_call(
        body,
        grid=(size // step,),
        in_specs=[
            pl.BlockSpec((tokens, step), lambda i: (0, first_column + i)),
            pl.BlockSpec((tokens, depth), lambda i: (0, 0)),
            pl.BlockSpec((step, depth), lambda i: (first + i, 0)),
        ]
        + [pl.BlockSpec(memory_space=pl.ANY)] * len(gates),
        out_specs=pl.BlockSpec((step, depth), lambda i: (i, 0)),
        out_shape=jax.ShapeDtypeStruct((size, depth), jnp.bfloat16),
        compiler_params=params_of(24 * MIB),
        cost_estimate=cost_of(
            tokens * size * depth, 6 * size * depth + 2 * tokens * depth
        ),
        name="moment_rows",
    )(attended, grads, momentum, *gates)


def averaged_rows(
    rate, params, far_params, far_start, moment, far_moment, start, size, results
):
    depth = params.shape[1]
    step = math.gcd(size, HD if size > HD else HD // 2)
    first = start // step
    far_first = (start - far_start) // step

    def body(rate_ref, params_ref, far_params_ref, moment_ref, far_moment_ref, *refs):
        new_params_ref, new_momentum_ref = refs[-2:]
        mean_moment = 0.5 * (
            moment_ref[...].astype(jnp.float32) + far_moment_ref[...].astype(jnp.float32)
        )
        mean_params = 0.5 * (params_ref[...] + far_params_ref[...].astype(jnp.float32))
        new_momentum_ref[...] = mean_moment
        new_params_ref[...] = mean_params - rate_ref[0] * mean_moment

    whole_spec = pl.BlockSpec((step, depth), lambda i: (first + i, 0))
    part_spec = pl.BlockSpec((step, depth), lambda i: (i, 0))
    kept = [] if results is None else list(results)
    return pl.pallas_call(
        body,
        grid=(size // step,),
        in_specs=[
            pl.BlockSpec(memory_space=pltpu.SMEM),
            whole_spec,
            pl.BlockSpec((step, depth), lambda i: (far_first + i, 0)),
            part_spec,
            part_spec,
        ]
        + [pl.BlockSpec(memory_space=pl.ANY)] * len(kept),
        out_specs=[whole_spec] * 2,
        out_shape=[pltpu.HBM(params.shape, jnp.float32)] * 2,
        input_output_aliases={5 + i: i for i in range(len(kept))},
        compiler_params=params_of(16 * MIB),
        cost_estimate=cost_of(3 * size * depth, 18 * size * depth),
        name="averaged_rows",
    )(rate, params, far_params, moment, far_moment, *kept)


def placed_heads(place, pack, results, shift, count, group, groups):
    rows, width = results[0].shape
    span = width // count // groups

    def body(place_ref, pack_ref, *refs):
        for part in range(3):
            refs[3 + part][...] = pack_ref[part]

    spec = pl.BlockSpec(
        (rows, span),
        lambda i, place_ref: (0, lax.rem(place_ref[0] + shift, count) * groups + group),
    )
    return pl.pallas_call(
        body,
        grid_spec=pltpu.PrefetchScalarGridSpec(
            num_scalar_prefetch=1,
            grid=(1,),
            in_specs=[pl.BlockSpec((3, rows, span), lambda i, place_ref: (0, 0, 0))]
            + [pl.BlockSpec(memory_space=pl.ANY)] * 3,
            out_specs=[spec] * 3,
        ),
        out_shape=[pltpu.HBM((rows, width), jnp.bfloat16)] * 3,
        input_output_aliases={2 + part: part for part in range(3)},
        compiler_params=params_of(8 * MIB),
        cost_estimate=cost_of(0, 12 * rows * span),
        name="placed_heads",
    )(place, pack, *results)


def score_bias(me, count, own_ids, far_ids, block_mask):
    rows = own_ids.shape[0]
    blocks = block_mask.shape[0]
    block_rows = rows * count // blocks
    stems = jnp.concatenate([own_ids] + far_ids) // CODES
    position = jnp.concatenate(
        [lax.rem(me + count - s, count) * rows + jnp.arange(rows) for s in range(count)]
    )
    block_of = position // block_rows
    picks = (block_of[:, None] == jnp.arange(blocks)[None, :]).astype(jnp.float32)
    spread = jnp.dot(jnp.dot(picks, block_mask.astype(jnp.float32)), picks.T)
    allowed = (
        (spread > 0.5)
        & (position[None, :] <= position[:, None])
        & ((stems[:, None] == stems[None, :]) | (block_of[:, None] == block_of[None, :]))
    )
    return jnp.where(allowed, 0.0, -1e30)


def step_with_partner(
    bit_level,
    query_rows,
    key_rows,
    value_rows,
    out_grad,
    params,
    momentum,
    token_ids,
    block_mask,
    rate,
):
    count = lax.axis_size("fsdp")
    me = lax.axis_index("fsdp")
    place = me.astype(jnp.int32).reshape(1)
    local, inner = params.shape[0], params.shape[0] * count
    route = partner_route(lax.axis_size("dp"), bit_level)
    shifts = range(1, count)
    near = bit_level == 0
    groups = math.gcd(local // HD, 2) if near else 1
    span = local // groups
    if near:
        chunks = [[(group * span, span)] for group in range(groups)]
    else:
        chunks = [row_chunks(group * span, span) for group in range(groups)]

    tensors = (query_rows, key_rows, value_rows)
    rings = [shift_route(count, shift) for shift in shifts]
    far_params = []
    read_params = params
    if not near:
        read_params = in_hbm(params)
        cut = chunks[0][-2][0] if len(chunks[0]) > 2 else local
        for start, size in ((0, cut), (cut, local - cut)):
            if size:
                short = short_rows(read_params, start, size)
                far_params.append((start, size, lax.ppermute(short, "dp", route)))

    packs, ids_sent = [], token_ids
    for group in range(groups):
        packs.append([])
        for shift, ring in zip(shifts, rings):
            pack, ids_copy = packed_heads(
                place, tensors, out_grad, token_ids, shift, count, group, groups
            )
            packs[group].append(lax.ppermute(pack, "fsdp", ring))
            if not near:
                ids_sent = ids_copy
    far_ids = [lax.ppermute(ids_sent, "fsdp", ring) for ring in rings]

    bias = score_bias(me, count, token_ids, far_ids, block_mask)
    attended, returned, results, grads = [], [], None, out_grad
    for group in range(groups):
        outs = attention_step(
            place,
            bias,
            tensors,
            packs[group],
            grads,
            read_params,
            results,
            count,
            group,
            groups,
            near,
        )
        attended.append(outs[0])
        results, backs = outs[1:4], outs[4 : 4 + len(shifts)]
        if group == 0:
            grads = outs[4 + len(shifts)]
        if near:
            far = lax.ppermute(outs[-1], "dp", route)
            far_params.append((group * span, span, far))
        returned.append(
            [
                lax.ppermute(back, "fsdp", shift_route(count, -shift))
                for shift, back in zip(shifts, backs)
            ]
        )
    sent = []
    for group in range(groups):
        gates = returned[0][:1] if group else []
        for start, size in chunks[group]:
            moment = moment_rows(
                attended[group], grads, momentum, start, size, group * span, inner, gates
            )
            sent.append((start, size, moment, lax.ppermute(moment, "dp", route)))
    means = None
    for start, size, moment, far_moment in sent:
        far_start, far = next(
            (first, rows) for first, many, rows in far_params if first <= start < first + many
        )
        means = averaged_rows(
            rate,
            params,
            far,
            far_start,
            moment,
            far_moment,
            start,
            size,
            means,
        )
    for group in range(groups):
        for shift, pack in zip(shifts, returned[group]):
            results = placed_heads(place, pack, results, shift, count, group, groups)
    return (*results, *means)


def shards(
    query_rows, key_rows, value_rows, out_grad, params, momentum, token_ids, block_mask, step_index
):
    step_value = step_index[0]
    correction = 1.0 / (
        1.0 - jnp.exp((step_value + 1).astype(jnp.float32) * math.log(MOMENTUM_RATE))
    )
    rate = (LEARN_RATE * correction).reshape(1)
    return lax.switch(
        step_value % 4,
        [functools.partial(step_with_partner, bit_level) for bit_level in range(4)],
        query_rows,
        key_rows,
        value_rows,
        out_grad,
        params,
        momentum,
        token_ids,
        block_mask,
        rate,
    )


def solution(mesh):
    rows = P(("dp", "fsdp"), None)
    return jax.shard_map(
        shards,
        mesh=mesh,
        in_specs=(rows,) * 6 + (P(("dp", "fsdp")), P(), P()),
        out_specs=(rows,) * 5,
        check_vma=False,
    )
```

```python
import functools
import math

import jax
import jax.numpy as jnp
from jax import lax
from jax.experimental import pallas as pl
from jax.experimental.pallas import tpu as pltpu
from jax.sharding import PartitionSpec as P

HD = 128
CODES = 2048
MOMENTUM_RATE = 0.9
LEARN_RATE = 0.25
MIB = 1 << 20

CONTRACT_LAST = (((1,), (1,)), ((), ()))
CONTRACT_FIRST = (((0,), (0,)), ((), ()))


def dot_f32(left, right, dims):
    return lax.dot_general(left, right, dims, preferred_element_type=jnp.float32)


def cost_of(macs, moved):
    return pl.CostEstimate(flops=2 * macs, bytes_accessed=moved, transcendentals=0)


def params_of(limit):
    return pltpu.CompilerParams(vmem_limit_bytes=limit)


def row_chunks(start, rows):
    chunks, end = [], start + rows
    while start < end:
        left = (end - start) // HD
        size = HD * (left // 2 if left > 2 else 1)
        chunks.append((start, size))
        start += size
    return chunks


def in_hbm(array):
    return pltpu.with_memory_space_constraint(array, pltpu.HBM)


def partner_route(count, bit_level):
    route = []
    for low in range(count):
        high = low | 1 << bit_level
        if high != low and high < count:
            route += [(low, high), (high, low)]
    return route


def shift_route(count, shift):
    return [(source, (source + shift) % count) for source in range(count)]


def short_rows(params, start, size):
    width = params.shape[1]
    piece = math.gcd(size, HD)
    pieces = size // piece

    def body(wide_ref, short_ref, wide, short, in_sem, out_sem):
        reads = [
            pltpu.make_async_copy(
                wide_ref.at[pl.ds(start + i * piece, piece)], wide.at[i], in_sem.at[i]
            )
            for i in range(pieces)
        ]
        writes = [
            pltpu.make_async_copy(
                short.at[i], short_ref.at[pl.ds(i * piece, piece)], out_sem.at[i]
            )
            for i in range(pieces)
        ]
        for read in reads:
            read.start()
        for i in range(pieces):
            reads[i].wait()
            short[i] = wide[i].astype(jnp.bfloat16)
            writes[i].start()
        for write in writes:
            write.wait()

    return pl.pallas_call(
        body,
        in_specs=[pl.BlockSpec(memory_space=pl.ANY)],
        out_specs=pl.BlockSpec(memory_space=pl.ANY),
        out_shape=jax.ShapeDtypeStruct((size, width), jnp.bfloat16),
        scratch_shapes=[
            pltpu.VMEM((pieces, piece, width), jnp.float32),
            pltpu.VMEM((pieces, piece, width), jnp.bfloat16),
            pltpu.SemaphoreType.DMA((pieces,)),
            pltpu.SemaphoreType.DMA((pieces,)),
        ],
        compiler_params=params_of(6 * size * width + 2 * MIB),
        cost_estimate=cost_of(0, 6 * size * width),
        name="short_rows",
    )(params)


def packed_heads(place, tensors, out_grad, token_ids, shift, count, group, groups):
    rows, width = tensors[0].shape
    span = width // count // groups
    slabs = out_grad.shape[1] // span if group == 0 else 0

    def body(place_ref, query_ref, key_ref, value_ref, *refs):
        pack_ref = refs[-2] if slabs else refs[-1]
        for slab in range(slabs):
            pack_ref[slab] = refs[0][:, slab * span : (slab + 1) * span]
        if slabs:
            refs[-1][...] = refs[1][...]
        pack_ref[slabs] = query_ref[...]
        pack_ref[slabs + 1] = key_ref[...]
        pack_ref[slabs + 2] = value_ref[...]

    spec = pl.BlockSpec(
        (rows, span),
        lambda i, place_ref: (0, lax.rem(place_ref[0] + shift, count) * groups + group),
    )
    grad_spec = pl.BlockSpec(out_grad.shape, lambda i, place_ref: (0, 0))
    ids_spec = pl.BlockSpec((1, rows), lambda i, place_ref: (0, 0))
    outs = pl.pallas_call(
        body,
        grid_spec=pltpu.PrefetchScalarGridSpec(
            num_scalar_prefetch=1,
            grid=(1,),
            in_specs=[spec] * 3
            + [grad_spec, ids_spec] * (slabs > 0),
            out_specs=[
                pl.BlockSpec((slabs + 3, rows, span), lambda i, place_ref: (0, 0, 0))
            ]
            + [ids_spec] * (slabs > 0),
        ),
        out_shape=[jax.ShapeDtypeStruct((slabs + 3, rows, span), out_grad.dtype)]
        + [jax.ShapeDtypeStruct((1, rows), token_ids.dtype)] * (slabs > 0),
        compiler_params=params_of(12 * MIB),
        cost_estimate=cost_of(0, 4 * (slabs + 3) * rows * span),
        name="packed_heads",
    )(place, *tensors, *[out_grad, token_ids.reshape(1, rows)] * (slabs > 0))
    return outs[0], outs[1].reshape(rows) if slabs else None


def attention_step(
    place, bias, tensors, packs, grads, params, results, count, group, groups, short_out
):
    rows, width = tensors[0].shape
    tokens = rows * count
    heads = width // count // HD // groups
    together = math.gcd(heads, 2)
    span = together * HD
    steps = heads // together
    depth = params.shape[1]
    first = group == 0
    slabs = packs[0].shape[0] - 3 if packs else 0
    slab = heads * HD
    kept = [] if results is None else list(results)
    score_scale = 1.0 / math.sqrt(HD)
    inv_width = 1.0 / math.sqrt(width)
    far = count - 1

    def body(place_ref, bias_ref, query_ref, key_ref, value_ref, *refs):
        pack_refs, refs = [refs[3 * s : 3 * s + 3] for s in range(far)], refs[3 * far :]
        slab_refs, refs = refs[: far * first], refs[far * first :]
        grads_ref, params_ref = refs[:2]
        refs = refs[2 + len(kept) :]
        attended_ref, dq_ref, dk_ref, dv_ref = refs[:4]
        back_refs = refs[4 : 4 + far]

        if first:
            own_ref, grads_ref = grads_ref, refs[4 + far]

            @pl.when(pl.program_id(0) == 0)
            def _():
                grads_ref[:rows, :] = own_ref[...]
                for s in range(far):
                    for at in range(slabs):
                        grads_ref[
                            (s + 1) * rows : (s + 2) * rows, at * slab : (at + 1) * slab
                        ] = slab_refs[s][at]

        weight = params_ref[...].astype(jnp.bfloat16)
        if short_out:
            refs[-1][...] = weight
        grad_heads = (dot_f32(grads_ref[...], weight, CONTRACT_LAST) * inv_width).astype(
            jnp.bfloat16
        )
        for g in range(together):
            cols = slice(g * HD, (g + 1) * HD)

            def whole(own_ref, part):
                return jnp.concatenate(
                    [own_ref[:, cols]] + [far_refs[part][:, cols] for far_refs in pack_refs],
                    axis=0,
                )

            query, key, value = whole(query_ref, 0), whole(key_ref, 1), whole(value_ref, 2)
            grad = grad_heads[:, cols]
            scores = dot_f32(query, key, CONTRACT_LAST) * score_scale + bias_ref[...]
            top = jnp.max(scores, axis=-1, keepdims=True)
            terms = jnp.exp(scores - top)
            prob = terms * (1.0 / jnp.sum(terms, axis=-1, keepdims=True))
            prob16 = prob.astype(jnp.bfloat16)
            attended_ref[:, cols] = jnp.dot(
                prob16, value, preferred_element_type=jnp.float32
            ).astype(jnp.bfloat16)
            grad_value = dot_f32(prob16, grad, CONTRACT_FIRST).astype(jnp.bfloat16)
            grad_prob = dot_f32(grad, value, CONTRACT_LAST)
            row_dot = jnp.sum(prob * grad_prob, axis=-1, keepdims=True)
            grad_score = (prob * (grad_prob - row_dot) * score_scale).astype(jnp.bfloat16)
            grad_query = jnp.dot(
                grad_score, key, preferred_element_type=jnp.float32
            ).astype(jnp.bfloat16)
            grad_key = dot_f32(grad_score, query, CONTRACT_FIRST).astype(jnp.bfloat16)
            for part, (out_ref, result) in enumerate(
                ((dq_ref, grad_query), (dk_ref, grad_key), (dv_ref, grad_value))
            ):
                out_ref[:, cols] = result[:rows]
                for s in range(far):
                    back_refs[s][part, :, cols] = result[(s + 1) * rows : (s + 2) * rows]

    own_spec = pl.BlockSpec(
        (rows, span), lambda i, place_ref: (0, (place_ref[0] * groups + group) * steps + i)
    )
    pack_specs = [
        pl.BlockSpec((None, rows, span), lambda i, place_ref, part=part: (part, 0, i))
        for part in range(slabs, slabs + 3)
    ]
    back_spec = pl.BlockSpec((3, rows, span), lambda i, place_ref: (0, 0, i))
    all_spec = pl.BlockSpec((tokens, depth), lambda i, place_ref: (0, 0))
    own_shape = pltpu.HBM((rows, width), jnp.bfloat16)
    macs = tokens * depth * heads * HD + 5 * heads * tokens * tokens * HD
    operands = [place, bias, *tensors]
    for pack in packs:
        operands += [pack] * 3
    in_specs = (
        [pl.BlockSpec((tokens, tokens), lambda i, place_ref: (0, 0))]
        + [own_spec] * 3
        + pack_specs * far
    )
    if first:
        operands += packs
        in_specs += [
            pl.BlockSpec((slabs, rows, slab), lambda i, place_ref: (0, 0, 0))
        ] * far + [pl.BlockSpec((rows, depth), lambda i, place_ref: (0, 0))]
    else:
        in_specs += [all_spec]
    operands += [grads, params]
    in_specs += [pl.BlockSpec((span, depth), lambda i, place_ref: (group * steps + i, 0))]
    aliases = {len(operands) + i: 1 + i for i in range(len(kept))}
    in_specs += [pl.BlockSpec(memory_space=pl.ANY)] * len(kept)
    return pl.pallas_call(
        body,
        grid_spec=pltpu.PrefetchScalarGridSpec(
            num_scalar_prefetch=1,
            grid=(steps,),
            in_specs=in_specs,
            out_specs=[pl.BlockSpec((tokens, span), lambda i, place_ref: (0, i))]
            + [own_spec] * 3
            + [back_spec] * far
            + [all_spec] * first
            + [pl.BlockSpec((span, depth), lambda i, place_ref: (i, 0))] * short_out,
        ),
        out_shape=[jax.ShapeDtypeStruct((tokens, heads * HD), jnp.bfloat16)]
        + [own_shape] * 3
        + [jax.ShapeDtypeStruct((3, rows, heads * HD), jnp.bfloat16)] * far
        + [jax.ShapeDtypeStruct((tokens, depth), jnp.bfloat16)] * first
        + [jax.ShapeDtypeStruct((heads * HD, depth), jnp.bfloat16)] * short_out,
        input_output_aliases=aliases,
        compiler_params=params_of((24 if tokens <= 256 else 56) * MIB),
        cost_estimate=cost_of(macs, heads * HD * (4 * depth + 16 * tokens)),
        name="attention_step",
    )(*operands, *kept)


def moment_rows(attended, grads, momentum, start, size, group_start, inner, gates):
    tokens, depth = grads.shape
    step = math.gcd(size, 2 * HD)
    first = start // step
    first_column = (start - group_start) // step
    inv_width = 1.0 / math.sqrt(inner)


    def body(attended_ref, grads_ref, momentum_ref, *refs):
        total = dot_f32(attended_ref[...], grads_ref[...], CONTRACT_FIRST)
        refs[-1][...] = (
            MOMENTUM_RATE * momentum_ref[...] + total * inv_width
        ).astype(jnp.bfloat16)

    return pl.pallas_call(
        body,
        grid=(size // step,),
        in_specs=[
            pl.BlockSpec((tokens, step), lambda i: (0, first_column + i)),
            pl.BlockSpec((tokens, depth), lambda i: (0, 0)),
            pl.BlockSpec((step, depth), lambda i: (first + i, 0)),
        ]
        + [pl.BlockSpec(memory_space=pl.ANY)] * len(gates),
        out_specs=pl.BlockSpec((step, depth), lambda i: (i, 0)),
        out_shape=jax.ShapeDtypeStruct((size, depth), jnp.bfloat16),
        compiler_params=params_of(24 * MIB),
        cost_estimate=cost_of(
            tokens * size * depth, 6 * size * depth + 2 * tokens * depth
        ),
        name="moment_rows",
    )(attended, grads, momentum, *gates)


def averaged_rows(
    rate, params, far_params, far_start, moment, far_moment, start, size, results
):
    depth = params.shape[1]
    step = math.gcd(size, HD if size > HD else HD // 2)
    first = start // step
    far_first = (start - far_start) // step

    def body(rate_ref, params_ref, far_params_ref, moment_ref, far_moment_ref, *refs):
        new_params_ref, new_momentum_ref = refs[-2:]
        mean_moment = 0.5 * (
            moment_ref[...].astype(jnp.float32) + far_moment_ref[...].astype(jnp.float32)
        )
        mean_params = 0.5 * (params_ref[...] + far_params_ref[...].astype(jnp.float32))
        new_momentum_ref[...] = mean_moment
        new_params_ref[...] = mean_params - rate_ref[0] * mean_moment

    whole_spec = pl.BlockSpec((step, depth), lambda i: (first + i, 0))
    part_spec = pl.BlockSpec((step, depth), lambda i: (i, 0))
    kept = [] if results is None else list(results)
    return pl.pallas_call(
        body,
        grid=(size // step,),
        in_specs=[
            pl.BlockSpec(memory_space=pltpu.SMEM),
            whole_spec,
            pl.BlockSpec((step, depth), lambda i: (far_first + i, 0)),
            part_spec,
            part_spec,
        ]
        + [pl.BlockSpec(memory_space=pl.ANY)] * len(kept),
        out_specs=[whole_spec] * 2,
        out_shape=[pltpu.HBM(params.shape, jnp.float32)] * 2,
        input_output_aliases={5 + i: i for i in range(len(kept))},
        compiler_params=params_of(16 * MIB),
        cost_estimate=cost_of(3 * size * depth, 18 * size * depth),
        name="averaged_rows",
    )(rate, params, far_params, moment, far_moment, *kept)


def placed_heads(place, pack, results, shift, count, group, groups, gates):
    rows, width = results[0].shape
    span = width // count // groups

    def body(place_ref, pack_ref, *refs):
        for part in range(3):
            refs[len(refs) - 3 + part][...] = pack_ref[part]

    spec = pl.BlockSpec(
        (rows, span),
        lambda i, place_ref: (0, lax.rem(place_ref[0] + shift, count) * groups + group),
    )
    return pl.pallas_call(
        body,
        grid_spec=pltpu.PrefetchScalarGridSpec(
            num_scalar_prefetch=1,
            grid=(1,),
            in_specs=[pl.BlockSpec((3, rows, span), lambda i, place_ref: (0, 0, 0))]
            + [pl.BlockSpec(memory_space=pl.ANY)] * (3 + len(gates)),
            out_specs=[spec] * 3,
        ),
        out_shape=[pltpu.HBM((rows, width), jnp.bfloat16)] * 3,
        input_output_aliases={2 + part: part for part in range(3)},
        compiler_params=params_of(8 * MIB),
        cost_estimate=cost_of(0, 12 * rows * span),
        name="placed_heads",
    )(place, pack, *results, *gates)


def score_bias(me, count, own_ids, far_ids, block_mask):
    rows = own_ids.shape[0]
    blocks = block_mask.shape[0]
    block_rows = rows * count // blocks
    stems = jnp.concatenate([own_ids] + far_ids) // CODES
    position = jnp.concatenate(
        [lax.rem(me + count - s, count) * rows + jnp.arange(rows) for s in range(count)]
    )
    block_of = position // block_rows
    picks = (block_of[:, None] == jnp.arange(blocks)[None, :]).astype(jnp.float32)
    spread = jnp.dot(jnp.dot(picks, block_mask.astype(jnp.float32)), picks.T)
    allowed = (
        (spread > 0.5)
        & (position[None, :] <= position[:, None])
        & ((stems[:, None] == stems[None, :]) | (block_of[:, None] == block_of[None, :]))
    )
    return jnp.where(allowed, 0.0, -1e30)


def step_with_partner(
    bit_level,
    query_rows,
    key_rows,
    value_rows,
    out_grad,
    params,
    momentum,
    token_ids,
    block_mask,
    rate,
):
    count = lax.axis_size("fsdp")
    me = lax.axis_index("fsdp")
    place = me.astype(jnp.int32).reshape(1)
    local, inner = params.shape[0], params.shape[0] * count
    route = partner_route(lax.axis_size("dp"), bit_level)
    shifts = range(1, count)
    near = bit_level == 0
    groups = math.gcd(local // HD, 2) if near else 1
    span = local // groups
    if near:
        chunks = [[(group * span, span)] for group in range(groups)]
    else:
        chunks = [row_chunks(group * span, span) for group in range(groups)]

    tensors = (query_rows, key_rows, value_rows)
    rings = [shift_route(count, shift) for shift in shifts]
    far_params = []
    read_params = params
    if not near:
        read_params = in_hbm(params)
        cut = chunks[0][-2][0] if len(chunks[0]) > 2 else local
        for start, size in ((0, cut), (cut, local - cut)):
            if size:
                short = short_rows(read_params, start, size)
                far_params.append((start, size, lax.ppermute(short, "dp", route)))

    packs, ids_sent = [], token_ids
    for group in range(groups):
        packs.append([])
        for shift, ring in zip(shifts, rings):
            pack, ids_copy = packed_heads(
                place, tensors, out_grad, token_ids, shift, count, group, groups
            )
            packs[group].append(lax.ppermute(pack, "fsdp", ring))
            if not near:
                ids_sent = ids_copy
    far_ids = [lax.ppermute(ids_sent, "fsdp", ring) for ring in rings]

    bias = score_bias(me, count, token_ids, far_ids, block_mask)
    attended, returned, results, grads = [], [], None, out_grad
    for group in range(groups):
        outs = attention_step(
            place,
            bias,
            tensors,
            packs[group],
            grads,
            read_params,
            results,
            count,
            group,
            groups,
            near,
        )
        attended.append(outs[0])
        results, backs = outs[1:4], outs[4 : 4 + len(shifts)]
        if group == 0:
            grads = outs[4 + len(shifts)]
        if near:
            far = lax.ppermute(outs[-1], "dp", route)
            far_params.append((group * span, span, far))
        returned.append(
            [
                lax.ppermute(back, "fsdp", shift_route(count, -shift))
                for shift, back in zip(shifts, backs)
            ]
        )
    sent = []
    for group in range(groups):
        gates = returned[0][:1] if group else []
        for start, size in chunks[group]:
            moment = moment_rows(
                attended[group], grads, momentum, start, size, group * span, inner, gates
            )
            sent.append((start, size, moment, lax.ppermute(moment, "dp", route)))
    means = None
    for start, size, moment, far_moment in sent:
        far_start, far = next(
            (first, rows) for first, many, rows in far_params if first <= start < first + many
        )
        means = averaged_rows(
            rate,
            params,
            far,
            far_start,
            moment,
            far_moment,
            start,
            size,
            means,
        )
    for group in range(groups):
        gates = means[:1] if group else []
        for shift, pack in zip(shifts, returned[group]):
            results = placed_heads(place, pack, results, shift, count, group, groups, gates)
    return (*results, *means)


def shards(
    query_rows, key_rows, value_rows, out_grad, params, momentum, token_ids, block_mask, step_index
):
    step_value = step_index[0]
    correction = 1.0 / (
        1.0 - jnp.exp((step_value + 1).astype(jnp.float32) * math.log(MOMENTUM_RATE))
    )
    rate = (LEARN_RATE * correction).reshape(1)
    return lax.switch(
        step_value % 4,
        [functools.partial(step_with_partner, bit_level) for bit_level in range(4)],
        query_rows,
        key_rows,
        value_rows,
        out_grad,
        params,
        momentum,
        token_ids,
        block_mask,
        rate,
    )


def solution(mesh):
    rows = P(("dp", "fsdp"), None)
    return jax.shard_map(
        shards,
        mesh=mesh,
        in_specs=(rows,) * 6 + (P(("dp", "fsdp")), P(), P()),
        out_specs=(rows,) * 5,
        check_vma=False,
    )
```

```python
import functools
import math

import jax
import jax.numpy as jnp
from jax import lax
from jax.experimental import pallas as pl
from jax.experimental.pallas import tpu as pltpu
from jax.sharding import PartitionSpec as P

HD = 128
CODES = 2048
MOMENTUM_RATE = 0.9
LEARN_RATE = 0.25
MIB = 1 << 20

CONTRACT_LAST = (((1,), (1,)), ((), ()))
CONTRACT_FIRST = (((0,), (0,)), ((), ()))


def dot_f32(left, right, dims):
    return lax.dot_general(left, right, dims, preferred_element_type=jnp.float32)


def cost_of(macs, moved):
    return pl.CostEstimate(flops=2 * macs, bytes_accessed=moved, transcendentals=0)


def params_of(limit):
    return pltpu.CompilerParams(vmem_limit_bytes=limit)


def row_chunks(start, rows):
    units = rows // HD
    if units < 8:
        sizes = [1] * units
    else:
        part = units // 8
        sizes = [units - 4 * part, 2 * part, part, part]
    chunks = []
    for size in sizes:
        chunks.append((start, size * HD))
        start += size * HD
    return chunks


def in_hbm(array):
    return pltpu.with_memory_space_constraint(array, pltpu.HBM)


def partner_route(count, bit_level):
    route = []
    for low in range(count):
        high = low | 1 << bit_level
        if high != low and high < count:
            route += [(low, high), (high, low)]
    return route


def shift_route(count, shift):
    return [(source, (source + shift) % count) for source in range(count)]


def short_rows(params, start, size):
    width = params.shape[1]
    piece = math.gcd(size, HD)
    pieces = size // piece

    def body(wide_ref, short_ref, wide, short, in_sem, out_sem):
        reads = [
            pltpu.make_async_copy(
                wide_ref.at[pl.ds(start + i * piece, piece)], wide.at[i], in_sem.at[i]
            )
            for i in range(pieces)
        ]
        writes = [
            pltpu.make_async_copy(
                short.at[i], short_ref.at[pl.ds(i * piece, piece)], out_sem.at[i]
            )
            for i in range(pieces)
        ]
        for read in reads:
            read.start()
        for i in range(pieces):
            reads[i].wait()
            short[i] = wide[i].astype(jnp.bfloat16)
            writes[i].start()
        for write in writes:
            write.wait()

    return pl.pallas_call(
        body,
        in_specs=[pl.BlockSpec(memory_space=pl.ANY)],
        out_specs=pl.BlockSpec(memory_space=pl.ANY),
        out_shape=jax.ShapeDtypeStruct((size, width), jnp.bfloat16),
        scratch_shapes=[
            pltpu.VMEM((pieces, piece, width), jnp.float32),
            pltpu.VMEM((pieces, piece, width), jnp.bfloat16),
            pltpu.SemaphoreType.DMA((pieces,)),
            pltpu.SemaphoreType.DMA((pieces,)),
        ],
        compiler_params=params_of(6 * size * width + 2 * MIB),
        cost_estimate=cost_of(0, 6 * size * width),
        name="short_rows",
    )(params)


def packed_heads(place, tensors, out_grad, token_ids, shift, count, group, groups):
    rows, width = tensors[0].shape
    span = width // count // groups
    slabs = out_grad.shape[1] // span if group == 0 else 0

    def body(place_ref, query_ref, key_ref, value_ref, *refs):
        pack_ref = refs[-2] if slabs else refs[-1]
        for slab in range(slabs):
            pack_ref[slab] = refs[0][:, slab * span : (slab + 1) * span]
        if slabs:
            refs[-1][...] = refs[1][...]
        pack_ref[slabs] = query_ref[...]
        pack_ref[slabs + 1] = key_ref[...]
        pack_ref[slabs + 2] = value_ref[...]

    spec = pl.BlockSpec(
        (rows, span),
        lambda i, place_ref: (0, lax.rem(place_ref[0] + shift, count) * groups + group),
    )
    grad_spec = pl.BlockSpec(out_grad.shape, lambda i, place_ref: (0, 0))
    ids_spec = pl.BlockSpec((1, rows), lambda i, place_ref: (0, 0))
    outs = pl.pallas_call(
        body,
        grid_spec=pltpu.PrefetchScalarGridSpec(
            num_scalar_prefetch=1,
            grid=(1,),
            in_specs=[spec] * 3
            + [grad_spec, ids_spec] * (slabs > 0),
            out_specs=[
                pl.BlockSpec((slabs + 3, rows, span), lambda i, place_ref: (0, 0, 0))
            ]
            + [ids_spec] * (slabs > 0),
        ),
        out_shape=[jax.ShapeDtypeStruct((slabs + 3, rows, span), out_grad.dtype)]
        + [jax.ShapeDtypeStruct((1, rows), token_ids.dtype)] * (slabs > 0),
        compiler_params=params_of(12 * MIB),
        cost_estimate=cost_of(0, 4 * (slabs + 3) * rows * span),
        name="packed_heads",
    )(place, *tensors, *[out_grad, token_ids.reshape(1, rows)] * (slabs > 0))
    return outs[0], outs[1].reshape(rows) if slabs else None


def attention_step(
    place, bias, tensors, packs, grads, params, results, count, group, groups, short_out
):
    rows, width = tensors[0].shape
    tokens = rows * count
    heads = width // count // HD // groups
    together = math.gcd(heads, 2)
    span = together * HD
    steps = heads // together
    depth = params.shape[1]
    first = group == 0
    slabs = packs[0].shape[0] - 3 if packs else 0
    slab = heads * HD
    kept = [] if results is None else list(results)
    score_scale = 1.0 / math.sqrt(HD)
    inv_width = 1.0 / math.sqrt(width)
    far = count - 1

    def body(place_ref, bias_ref, query_ref, key_ref, value_ref, *refs):
        pack_refs, refs = [refs[3 * s : 3 * s + 3] for s in range(far)], refs[3 * far :]
        slab_refs, refs = refs[: far * first], refs[far * first :]
        grads_ref, params_ref = refs[:2]
        refs = refs[2 + len(kept) :]
        attended_ref, dq_ref, dk_ref, dv_ref = refs[:4]
        back_refs = refs[4 : 4 + far]

        if first:
            own_ref, grads_ref = grads_ref, refs[4 + far]

            @pl.when(pl.program_id(0) == 0)
            def _():
                grads_ref[:rows, :] = own_ref[...]
                for s in range(far):
                    for at in range(slabs):
                        grads_ref[
                            (s + 1) * rows : (s + 2) * rows, at * slab : (at + 1) * slab
                        ] = slab_refs[s][at]

        weight = params_ref[...].astype(jnp.bfloat16)
        if short_out:
            refs[-1][...] = weight
        grad_heads = (dot_f32(grads_ref[...], weight, CONTRACT_LAST) * inv_width).astype(
            jnp.bfloat16
        )
        for g in range(together):
            cols = slice(g * HD, (g + 1) * HD)

            def whole(own_ref, part):
                return jnp.concatenate(
                    [own_ref[:, cols]] + [far_refs[part][:, cols] for far_refs in pack_refs],
                    axis=0,
                )

            query, key, value = whole(query_ref, 0), whole(key_ref, 1), whole(value_ref, 2)
            grad = grad_heads[:, cols]
            scores = dot_f32(query, key, CONTRACT_LAST) * score_scale + bias_ref[...]
            top = jnp.max(scores, axis=-1, keepdims=True)
            terms = jnp.exp(scores - top)
            prob = terms * (1.0 / jnp.sum(terms, axis=-1, keepdims=True))
            prob16 = prob.astype(jnp.bfloat16)
            attended_ref[:, cols] = jnp.dot(
                prob16, value, preferred_element_type=jnp.float32
            ).astype(jnp.bfloat16)
            grad_value = dot_f32(prob16, grad, CONTRACT_FIRST).astype(jnp.bfloat16)
            grad_prob = dot_f32(grad, value, CONTRACT_LAST)
            row_dot = jnp.sum(prob * grad_prob, axis=-1, keepdims=True)
            grad_score = (prob * (grad_prob - row_dot) * score_scale).astype(jnp.bfloat16)
            grad_query = jnp.dot(
                grad_score, key, preferred_element_type=jnp.float32
            ).astype(jnp.bfloat16)
            grad_key = dot_f32(grad_score, query, CONTRACT_FIRST).astype(jnp.bfloat16)
            for part, (out_ref, result) in enumerate(
                ((dq_ref, grad_query), (dk_ref, grad_key), (dv_ref, grad_value))
            ):
                out_ref[:, cols] = result[:rows]
                for s in range(far):
                    back_refs[s][part, :, cols] = result[(s + 1) * rows : (s + 2) * rows]

    own_spec = pl.BlockSpec(
        (rows, span), lambda i, place_ref: (0, (place_ref[0] * groups + group) * steps + i)
    )
    pack_specs = [
        pl.BlockSpec((None, rows, span), lambda i, place_ref, part=part: (part, 0, i))
        for part in range(slabs, slabs + 3)
    ]
    back_spec = pl.BlockSpec((3, rows, span), lambda i, place_ref: (0, 0, i))
    all_spec = pl.BlockSpec((tokens, depth), lambda i, place_ref: (0, 0))
    own_shape = pltpu.HBM((rows, width), jnp.bfloat16)
    macs = tokens * depth * heads * HD + 5 * heads * tokens * tokens * HD
    operands = [place, bias, *tensors]
    for pack in packs:
        operands += [pack] * 3
    in_specs = (
        [pl.BlockSpec((tokens, tokens), lambda i, place_ref: (0, 0))]
        + [own_spec] * 3
        + pack_specs * far
    )
    if first:
        operands += packs
        in_specs += [
            pl.BlockSpec((slabs, rows, slab), lambda i, place_ref: (0, 0, 0))
        ] * far + [pl.BlockSpec((rows, depth), lambda i, place_ref: (0, 0))]
    else:
        in_specs += [all_spec]
    operands += [grads, params]
    in_specs += [pl.BlockSpec((span, depth), lambda i, place_ref: (group * steps + i, 0))]
    aliases = {len(operands) + i: 1 + i for i in range(len(kept))}
    in_specs += [pl.BlockSpec(memory_space=pl.ANY)] * len(kept)
    return pl.pallas_call(
        body,
        grid_spec=pltpu.PrefetchScalarGridSpec(
            num_scalar_prefetch=1,
            grid=(steps,),
            in_specs=in_specs,
            out_specs=[pl.BlockSpec((tokens, span), lambda i, place_ref: (0, i))]
            + [own_spec] * 3
            + [back_spec] * far
            + [all_spec] * first
            + [pl.BlockSpec((span, depth), lambda i, place_ref: (i, 0))] * short_out,
        ),
        out_shape=[jax.ShapeDtypeStruct((tokens, heads * HD), jnp.bfloat16)]
        + [own_shape] * 3
        + [jax.ShapeDtypeStruct((3, rows, heads * HD), jnp.bfloat16)] * far
        + [jax.ShapeDtypeStruct((tokens, depth), jnp.bfloat16)] * first
        + [jax.ShapeDtypeStruct((heads * HD, depth), jnp.bfloat16)] * short_out,
        input_output_aliases=aliases,
        compiler_params=params_of((24 if tokens <= 256 else 56) * MIB),
        cost_estimate=cost_of(macs, heads * HD * (4 * depth + 16 * tokens)),
        name="attention_step",
    )(*operands, *kept)


def moment_rows(attended, grads, momentum, start, size, group_start, inner, gates):
    tokens, depth = grads.shape
    step = math.gcd(size, 2 * HD)
    first = start // step
    first_column = (start - group_start) // step
    inv_width = 1.0 / math.sqrt(inner)


    def body(attended_ref, grads_ref, momentum_ref, *refs):
        total = dot_f32(attended_ref[...], grads_ref[...], CONTRACT_FIRST)
        refs[-1][...] = (
            MOMENTUM_RATE * momentum_ref[...] + total * inv_width
        ).astype(jnp.bfloat16)

    return pl.pallas_call(
        body,
        grid=(size // step,),
        in_specs=[
            pl.BlockSpec((tokens, step), lambda i: (0, first_column + i)),
            pl.BlockSpec((tokens, depth), lambda i: (0, 0)),
            pl.BlockSpec((step, depth), lambda i: (first + i, 0)),
        ]
        + [pl.BlockSpec(memory_space=pl.ANY)] * len(gates),
        out_specs=pl.BlockSpec((step, depth), lambda i: (i, 0)),
        out_shape=jax.ShapeDtypeStruct((size, depth), jnp.bfloat16),
        compiler_params=params_of(24 * MIB),
        cost_estimate=cost_of(
            tokens * size * depth, 6 * size * depth + 2 * tokens * depth
        ),
        name="moment_rows",
    )(attended, grads, momentum, *gates)


def averaged_rows(
    rate, params, far_params, far_start, moment, far_moment, start, size, results
):
    depth = params.shape[1]
    step = math.gcd(size, HD if size > HD else HD // 2)
    first = start // step
    far_first = (start - far_start) // step

    def body(rate_ref, params_ref, far_params_ref, moment_ref, far_moment_ref, *refs):
        new_params_ref, new_momentum_ref = refs[-2:]
        mean_moment = 0.5 * (
            moment_ref[...].astype(jnp.float32) + far_moment_ref[...].astype(jnp.float32)
        )
        mean_params = 0.5 * (params_ref[...] + far_params_ref[...].astype(jnp.float32))
        new_momentum_ref[...] = mean_moment
        new_params_ref[...] = mean_params - rate_ref[0] * mean_moment

    whole_spec = pl.BlockSpec((step, depth), lambda i: (first + i, 0))
    part_spec = pl.BlockSpec((step, depth), lambda i: (i, 0))
    kept = [] if results is None else list(results)
    return pl.pallas_call(
        body,
        grid=(size // step,),
        in_specs=[
            pl.BlockSpec(memory_space=pltpu.SMEM),
            whole_spec,
            pl.BlockSpec((step, depth), lambda i: (far_first + i, 0)),
            part_spec,
            part_spec,
        ]
        + [pl.BlockSpec(memory_space=pl.ANY)] * len(kept),
        out_specs=[whole_spec] * 2,
        out_shape=[pltpu.HBM(params.shape, jnp.float32)] * 2,
        input_output_aliases={5 + i: i for i in range(len(kept))},
        compiler_params=params_of(16 * MIB),
        cost_estimate=cost_of(3 * size * depth, 18 * size * depth),
        name="averaged_rows",
    )(rate, params, far_params, moment, far_moment, *kept)


def placed_heads(place, pack, results, shift, count, group, groups, gates):
    rows, width = results[0].shape
    span = width // count // groups

    def body(place_ref, pack_ref, *refs):
        for part in range(3):
            refs[len(refs) - 3 + part][...] = pack_ref[part]

    spec = pl.BlockSpec(
        (rows, span),
        lambda i, place_ref: (0, lax.rem(place_ref[0] + shift, count) * groups + group),
    )
    return pl.pallas_call(
        body,
        grid_spec=pltpu.PrefetchScalarGridSpec(
            num_scalar_prefetch=1,
            grid=(1,),
            in_specs=[pl.BlockSpec((3, rows, span), lambda i, place_ref: (0, 0, 0))]
            + [pl.BlockSpec(memory_space=pl.ANY)] * (3 + len(gates)),
            out_specs=[spec] * 3,
        ),
        out_shape=[pltpu.HBM((rows, width), jnp.bfloat16)] * 3,
        input_output_aliases={2 + part: part for part in range(3)},
        compiler_params=params_of(8 * MIB),
        cost_estimate=cost_of(0, 12 * rows * span),
        name="placed_heads",
    )(place, pack, *results, *gates)


def score_bias(me, count, own_ids, far_ids, block_mask):
    rows = own_ids.shape[0]
    blocks = block_mask.shape[0]
    block_rows = rows * count // blocks
    stems = jnp.concatenate([own_ids] + far_ids) // CODES
    position = jnp.concatenate(
        [lax.rem(me + count - s, count) * rows + jnp.arange(rows) for s in range(count)]
    )
    block_of = position // block_rows
    picks = (block_of[:, None] == jnp.arange(blocks)[None, :]).astype(jnp.float32)
    spread = jnp.dot(jnp.dot(picks, block_mask.astype(jnp.float32)), picks.T)
    allowed = (
        (spread > 0.5)
        & (position[None, :] <= position[:, None])
        & ((stems[:, None] == stems[None, :]) | (block_of[:, None] == block_of[None, :]))
    )
    return jnp.where(allowed, 0.0, -1e30)


def step_with_partner(
    bit_level,
    query_rows,
    key_rows,
    value_rows,
    out_grad,
    params,
    momentum,
    token_ids,
    block_mask,
    step_index,
):
    correction = 1.0 / (
        1.0 - jnp.exp((step_index[0] + 1).astype(jnp.float32) * math.log(MOMENTUM_RATE))
    )
    rate = (LEARN_RATE * correction).reshape(1)
    count = lax.axis_size("fsdp")
    me = lax.axis_index("fsdp")
    place = me.astype(jnp.int32).reshape(1)
    local, inner = params.shape[0], params.shape[0] * count
    route = partner_route(lax.axis_size("dp"), bit_level)
    shifts = range(1, count)
    near = bit_level == 0
    groups = math.gcd(local // HD, 2) if near else 1
    span = local // groups
    if near:
        chunks = [[(group * span, span)] for group in range(groups)]
    else:
        chunks = [row_chunks(group * span, span) for group in range(groups)]

    if not near:
        query_rows, key_rows, value_rows, out_grad = (
            in_hbm(rows) for rows in (query_rows, key_rows, value_rows, out_grad)
        )
    tensors = (query_rows, key_rows, value_rows)
    rings = [shift_route(count, shift) for shift in shifts]
    far_params = []
    read_params = params
    if not near:
        read_params = in_hbm(params)
        cut = chunks[0][-2][0] if len(chunks[0]) > 2 else local
        for start, size in ((0, cut), (cut, local - cut)):
            if size:
                short = short_rows(read_params, start, size)
                far_params.append((start, size, lax.ppermute(short, "dp", route)))

    packs, ids_sent = [], token_ids
    for group in range(groups):
        packs.append([])
        for shift, ring in zip(shifts, rings):
            pack, ids_copy = packed_heads(
                place, tensors, out_grad, token_ids, shift, count, group, groups
            )
            packs[group].append(lax.ppermute(pack, "fsdp", ring))
            if not near:
                ids_sent = ids_copy
    far_ids = [lax.ppermute(ids_sent, "fsdp", ring) for ring in rings]

    bias = score_bias(me, count, token_ids, far_ids, block_mask)
    attended, returned, results, grads = [], [], None, out_grad
    for group in range(groups):
        outs = attention_step(
            place,
            bias,
            tensors,
            packs[group],
            grads,
            read_params,
            results,
            count,
            group,
            groups,
            near,
        )
        attended.append(outs[0])
        results, backs = outs[1:4], outs[4 : 4 + len(shifts)]
        if group == 0:
            grads = outs[4 + len(shifts)]
        if near:
            far = lax.ppermute(outs[-1], "dp", route)
            far_params.append((group * span, span, far))
        returned.append(
            [
                lax.ppermute(back, "fsdp", shift_route(count, -shift))
                for shift, back in zip(shifts, backs)
            ]
        )
    sent = []
    for group in range(groups):
        gates = returned[0][:1] if group else []
        for start, size in chunks[group]:
            moment = moment_rows(
                attended[group], grads, momentum, start, size, group * span, inner, gates
            )
            sent.append((start, size, moment, lax.ppermute(moment, "dp", route)))
    means = None
    for start, size, moment, far_moment in sent:
        far_start, far = next(
            (first, rows) for first, many, rows in far_params if first <= start < first + many
        )
        means = averaged_rows(
            rate,
            params,
            far,
            far_start,
            moment,
            far_moment,
            start,
            size,
            means,
        )
    for group in range(groups):
        gates = means[:1] if group else []
        for shift, pack in zip(shifts, returned[group]):
            results = placed_heads(place, pack, results, shift, count, group, groups, gates)
    return (*results, *means)


def shards(
    query_rows, key_rows, value_rows, out_grad, params, momentum, token_ids, block_mask, step_index
):
    return lax.switch(
        step_index[0] & 3,
        [functools.partial(step_with_partner, bit_level) for bit_level in range(4)],
        query_rows,
        key_rows,
        value_rows,
        out_grad,
        params,
        momentum,
        token_ids,
        block_mask,
        step_index,
    )


def solution(mesh):
    rows = P(("dp", "fsdp"), None)
    return jax.shard_map(
        shards,
        mesh=mesh,
        in_specs=(rows,) * 6 + (P(("dp", "fsdp")), P(), P()),
        out_specs=(rows,) * 5,
        check_vma=False,
    )
```

```python
import functools
import math

import jax
import jax.numpy as jnp
from jax import lax
from jax.experimental import pallas as pl
from jax.experimental.pallas import tpu as pltpu
from jax.sharding import PartitionSpec as P

HD = 128
CODES = 2048
MOMENTUM_RATE = 0.9
LEARN_RATE = 0.25
MIB = 1 << 20

CONTRACT_LAST = (((1,), (1,)), ((), ()))
CONTRACT_FIRST = (((0,), (0,)), ((), ()))


def dot_f32(left, right, dims):
    return lax.dot_general(left, right, dims, preferred_element_type=jnp.float32)


def cost_of(macs, moved):
    return pl.CostEstimate(flops=2 * macs, bytes_accessed=moved, transcendentals=0)


def params_of(limit):
    return pltpu.CompilerParams(vmem_limit_bytes=limit)


def row_chunks(start, rows):
    units = rows // HD
    if units < 8:
        sizes = [1] * units
    else:
        part = units // 8
        sizes = [units - 4 * part, 2 * part, part, part]
    chunks = []
    for size in sizes:
        chunks.append((start, size * HD))
        start += size * HD
    return chunks


def in_hbm(array):
    return pltpu.with_memory_space_constraint(array, pltpu.HBM)


def partner_route(count, bit_level):
    route = []
    for low in range(count):
        high = low | 1 << bit_level
        if high != low and high < count:
            route += [(low, high), (high, low)]
    return route


def shift_route(count, shift):
    return [(source, (source + shift) % count) for source in range(count)]


def short_rows(params, start, size):
    width = params.shape[1]
    piece = math.gcd(size, HD)
    pieces = size // piece

    def body(wide_ref, short_ref, wide, in_sem):
        at = pl.program_id(0)

        def read(i):
            return pltpu.make_async_copy(
                wide_ref.at[pl.ds(start + i * piece, piece)], wide.at[i], in_sem.at[i]
            )

        @pl.when(at == 0)
        def _():
            for i in range(pieces):
                read(i).start()

        read(at).wait()
        short_ref[...] = wide[at].astype(jnp.bfloat16)

    return pl.pallas_call(
        body,
        grid=(pieces,),
        in_specs=[pl.BlockSpec(memory_space=pl.ANY)],
        out_specs=pl.BlockSpec((piece, width), lambda i: (i, 0)),
        out_shape=jax.ShapeDtypeStruct((size, width), jnp.bfloat16),
        scratch_shapes=[
            pltpu.VMEM((pieces, piece, width), jnp.float32),
            pltpu.SemaphoreType.DMA((pieces,)),
        ],
        compiler_params=params_of(4 * size * width + 4 * MIB),
        cost_estimate=cost_of(0, 6 * size * width),
        name="short_rows",
    )(params)


def packed_heads(place, tensors, out_grad, token_ids, shift, count, group, groups):
    rows, width = tensors[0].shape
    span = width // count // groups
    slabs = out_grad.shape[1] // span if group == 0 else 0

    def body(place_ref, query_ref, key_ref, value_ref, *refs):
        pack_ref = refs[-2] if slabs else refs[-1]
        for slab in range(slabs):
            pack_ref[slab] = refs[0][:, slab * span : (slab + 1) * span]
        if slabs:
            refs[-1][...] = refs[1][...]
        pack_ref[slabs] = query_ref[...]
        pack_ref[slabs + 1] = key_ref[...]
        pack_ref[slabs + 2] = value_ref[...]

    spec = pl.BlockSpec(
        (rows, span),
        lambda i, place_ref: (0, lax.rem(place_ref[0] + shift, count) * groups + group),
    )
    grad_spec = pl.BlockSpec(out_grad.shape, lambda i, place_ref: (0, 0))
    ids_spec = pl.BlockSpec((1, rows), lambda i, place_ref: (0, 0))
    outs = pl.pallas_call(
        body,
        grid_spec=pltpu.PrefetchScalarGridSpec(
            num_scalar_prefetch=1,
            grid=(1,),
            in_specs=[spec] * 3
            + [grad_spec, ids_spec] * (slabs > 0),
            out_specs=[
                pl.BlockSpec((slabs + 3, rows, span), lambda i, place_ref: (0, 0, 0))
            ]
            + [ids_spec] * (slabs > 0),
        ),
        out_shape=[jax.ShapeDtypeStruct((slabs + 3, rows, span), out_grad.dtype)]
        + [jax.ShapeDtypeStruct((1, rows), token_ids.dtype)] * (slabs > 0),
        compiler_params=params_of(12 * MIB),
        cost_estimate=cost_of(0, 4 * (slabs + 3) * rows * span),
        name="packed_heads",
    )(place, *tensors, *[out_grad, token_ids.reshape(1, rows)] * (slabs > 0))
    return outs[0], outs[1].reshape(rows) if slabs else None


def attention_step(
    place, bias, tensors, packs, grads, params, results, count, group, groups, short_out
):
    rows, width = tensors[0].shape
    tokens = rows * count
    heads = width // count // HD // groups
    together = math.gcd(heads, 2)
    span = together * HD
    steps = heads // together
    depth = params.shape[1]
    first = group == 0
    slabs = packs[0].shape[0] - 3 if packs else 0
    slab = heads * HD
    kept = [] if results is None else list(results)
    score_scale = 1.0 / math.sqrt(HD)
    inv_width = 1.0 / math.sqrt(width)
    far = count - 1

    def body(place_ref, bias_ref, query_ref, key_ref, value_ref, *refs):
        pack_refs, refs = [refs[3 * s : 3 * s + 3] for s in range(far)], refs[3 * far :]
        slab_refs, refs = refs[: far * first], refs[far * first :]
        grads_ref, params_ref = refs[:2]
        refs = refs[2 + len(kept) :]
        attended_ref, dq_ref, dk_ref, dv_ref = refs[:4]
        back_refs = refs[4 : 4 + far]

        if first:
            own_ref, grads_ref = grads_ref, refs[4 + far]

            @pl.when(pl.program_id(0) == 0)
            def _():
                grads_ref[:rows, :] = own_ref[...]
                for s in range(far):
                    for at in range(slabs):
                        grads_ref[
                            (s + 1) * rows : (s + 2) * rows, at * slab : (at + 1) * slab
                        ] = slab_refs[s][at]

        weight = params_ref[...].astype(jnp.bfloat16)
        if short_out:
            refs[-1][...] = weight
        grad_heads = (dot_f32(grads_ref[...], weight, CONTRACT_LAST) * inv_width).astype(
            jnp.bfloat16
        )
        for g in range(together):
            cols = slice(g * HD, (g + 1) * HD)

            def whole(own_ref, part):
                return jnp.concatenate(
                    [own_ref[:, cols]] + [far_refs[part][:, cols] for far_refs in pack_refs],
                    axis=0,
                )

            query, key, value = whole(query_ref, 0), whole(key_ref, 1), whole(value_ref, 2)
            grad = grad_heads[:, cols]
            scores = dot_f32(query, key, CONTRACT_LAST) * score_scale + bias_ref[...]
            top = jnp.max(scores, axis=-1, keepdims=True)
            terms = jnp.exp(scores - top)
            prob = terms * (1.0 / jnp.sum(terms, axis=-1, keepdims=True))
            prob16 = prob.astype(jnp.bfloat16)
            attended_ref[:, cols] = jnp.dot(
                prob16, value, preferred_element_type=jnp.float32
            ).astype(jnp.bfloat16)
            grad_value = dot_f32(prob16, grad, CONTRACT_FIRST).astype(jnp.bfloat16)
            grad_prob = dot_f32(grad, value, CONTRACT_LAST)
            row_dot = jnp.sum(prob * grad_prob, axis=-1, keepdims=True)
            grad_score = (prob * (grad_prob - row_dot) * score_scale).astype(jnp.bfloat16)
            grad_query = jnp.dot(
                grad_score, key, preferred_element_type=jnp.float32
            ).astype(jnp.bfloat16)
            grad_key = dot_f32(grad_score, query, CONTRACT_FIRST).astype(jnp.bfloat16)
            for part, (out_ref, result) in enumerate(
                ((dq_ref, grad_query), (dk_ref, grad_key), (dv_ref, grad_value))
            ):
                out_ref[:, cols] = result[:rows]
                for s in range(far):
                    back_refs[s][part, :, cols] = result[(s + 1) * rows : (s + 2) * rows]

    own_spec = pl.BlockSpec(
        (rows, span), lambda i, place_ref: (0, (place_ref[0] * groups + group) * steps + i)
    )
    pack_specs = [
        pl.BlockSpec((None, rows, span), lambda i, place_ref, part=part: (part, 0, i))
        for part in range(slabs, slabs + 3)
    ]
    back_spec = pl.BlockSpec((3, rows, span), lambda i, place_ref: (0, 0, i))
    all_spec = pl.BlockSpec((tokens, depth), lambda i, place_ref: (0, 0))
    own_shape = pltpu.HBM((rows, width), jnp.bfloat16)
    macs = tokens * depth * heads * HD + 5 * heads * tokens * tokens * HD
    operands = [place, bias, *tensors]
    for pack in packs:
        operands += [pack] * 3
    in_specs = (
        [pl.BlockSpec((tokens, tokens), lambda i, place_ref: (0, 0))]
        + [own_spec] * 3
        + pack_specs * far
    )
    if first:
        operands += packs
        in_specs += [
            pl.BlockSpec((slabs, rows, slab), lambda i, place_ref: (0, 0, 0))
        ] * far + [pl.BlockSpec((rows, depth), lambda i, place_ref: (0, 0))]
    else:
        in_specs += [all_spec]
    operands += [grads, params]
    in_specs += [pl.BlockSpec((span, depth), lambda i, place_ref: (group * steps + i, 0))]
    aliases = {len(operands) + i: 1 + i for i in range(len(kept))}
    in_specs += [pl.BlockSpec(memory_space=pl.ANY)] * len(kept)
    return pl.pallas_call(
        body,
        grid_spec=pltpu.PrefetchScalarGridSpec(
            num_scalar_prefetch=1,
            grid=(steps,),
            in_specs=in_specs,
            out_specs=[pl.BlockSpec((tokens, span), lambda i, place_ref: (0, i))]
            + [own_spec] * 3
            + [back_spec] * far
            + [all_spec] * first
            + [pl.BlockSpec((span, depth), lambda i, place_ref: (i, 0))] * short_out,
        ),
        out_shape=[jax.ShapeDtypeStruct((tokens, heads * HD), jnp.bfloat16)]
        + [own_shape] * 3
        + [jax.ShapeDtypeStruct((3, rows, heads * HD), jnp.bfloat16)] * far
        + [jax.ShapeDtypeStruct((tokens, depth), jnp.bfloat16)] * first
        + [jax.ShapeDtypeStruct((heads * HD, depth), jnp.bfloat16)] * short_out,
        input_output_aliases=aliases,
        compiler_params=params_of((24 if tokens <= 256 else 56) * MIB),
        cost_estimate=cost_of(macs, heads * HD * (4 * depth + 16 * tokens)),
        name="attention_step",
    )(*operands, *kept)


def moment_rows(attended, grads, momentum, start, size, group_start, inner, gates):
    tokens, depth = grads.shape
    step = math.gcd(size, 2 * HD)
    first = start // step
    first_column = (start - group_start) // step
    inv_width = 1.0 / math.sqrt(inner)


    def body(attended_ref, grads_ref, momentum_ref, *refs):
        total = dot_f32(attended_ref[...], grads_ref[...], CONTRACT_FIRST)
        refs[-1][...] = (
            MOMENTUM_RATE * momentum_ref[...] + total * inv_width
        ).astype(jnp.bfloat16)

    return pl.pallas_call(
        body,
        grid=(size // step,),
        in_specs=[
            pl.BlockSpec((tokens, step), lambda i: (0, first_column + i)),
            pl.BlockSpec((tokens, depth), lambda i: (0, 0)),
            pl.BlockSpec((step, depth), lambda i: (first + i, 0)),
        ]
        + [pl.BlockSpec(memory_space=pl.ANY)] * len(gates),
        out_specs=pl.BlockSpec((step, depth), lambda i: (i, 0)),
        out_shape=jax.ShapeDtypeStruct((size, depth), jnp.bfloat16),
        compiler_params=params_of(24 * MIB),
        cost_estimate=cost_of(
            tokens * size * depth, 6 * size * depth + 2 * tokens * depth
        ),
        name="moment_rows",
    )(attended, grads, momentum, *gates)


def averaged_rows(
    rate, params, far_params, far_start, moment, far_moment, start, size, results
):
    depth = params.shape[1]
    step = math.gcd(size, HD if size > HD else HD // 2)
    first = start // step
    far_first = (start - far_start) // step

    def body(rate_ref, params_ref, far_params_ref, moment_ref, far_moment_ref, *refs):
        new_params_ref, new_momentum_ref = refs[-2:]
        mean_moment = 0.5 * (
            moment_ref[...].astype(jnp.float32) + far_moment_ref[...].astype(jnp.float32)
        )
        mean_params = 0.5 * (params_ref[...] + far_params_ref[...].astype(jnp.float32))
        new_momentum_ref[...] = mean_moment
        new_params_ref[...] = mean_params - rate_ref[0] * mean_moment

    whole_spec = pl.BlockSpec((step, depth), lambda i: (first + i, 0))
    part_spec = pl.BlockSpec((step, depth), lambda i: (i, 0))
    kept = [] if results is None else list(results)
    return pl.pallas_call(
        body,
        grid=(size // step,),
        in_specs=[
            pl.BlockSpec(memory_space=pltpu.SMEM),
            whole_spec,
            pl.BlockSpec((step, depth), lambda i: (far_first + i, 0)),
            part_spec,
            part_spec,
        ]
        + [pl.BlockSpec(memory_space=pl.ANY)] * len(kept),
        out_specs=[whole_spec] * 2,
        out_shape=[pltpu.HBM(params.shape, jnp.float32)] * 2,
        input_output_aliases={5 + i: i for i in range(len(kept))},
        compiler_params=params_of(16 * MIB),
        cost_estimate=cost_of(3 * size * depth, 18 * size * depth),
        name="averaged_rows",
    )(rate, params, far_params, moment, far_moment, *kept)


def placed_heads(place, pack, results, shift, count, group, groups, gates):
    rows, width = results[0].shape
    span = width // count // groups

    def body(place_ref, pack_ref, *refs):
        for part in range(3):
            refs[len(refs) - 3 + part][...] = pack_ref[part]

    spec = pl.BlockSpec(
        (rows, span),
        lambda i, place_ref: (0, lax.rem(place_ref[0] + shift, count) * groups + group),
    )
    return pl.pallas_call(
        body,
        grid_spec=pltpu.PrefetchScalarGridSpec(
            num_scalar_prefetch=1,
            grid=(1,),
            in_specs=[pl.BlockSpec((3, rows, span), lambda i, place_ref: (0, 0, 0))]
            + [pl.BlockSpec(memory_space=pl.ANY)] * (3 + len(gates)),
            out_specs=[spec] * 3,
        ),
        out_shape=[pltpu.HBM((rows, width), jnp.bfloat16)] * 3,
        input_output_aliases={2 + part: part for part in range(3)},
        compiler_params=params_of(8 * MIB),
        cost_estimate=cost_of(0, 12 * rows * span),
        name="placed_heads",
    )(place, pack, *results, *gates)


def score_bias(me, count, own_ids, far_ids, block_mask):
    rows = own_ids.shape[0]
    blocks = block_mask.shape[0]
    block_rows = rows * count // blocks
    stems = jnp.concatenate([own_ids] + far_ids) // CODES
    position = jnp.concatenate(
        [lax.rem(me + count - s, count) * rows + jnp.arange(rows) for s in range(count)]
    )
    block_of = position // block_rows
    picks = (block_of[:, None] == jnp.arange(blocks)[None, :]).astype(jnp.float32)
    spread = jnp.dot(jnp.dot(picks, block_mask.astype(jnp.float32)), picks.T)
    allowed = (
        (spread > 0.5)
        & (position[None, :] <= position[:, None])
        & ((stems[:, None] == stems[None, :]) | (block_of[:, None] == block_of[None, :]))
    )
    return jnp.where(allowed, 0.0, -1e30)


def step_with_partner(
    bit_level,
    query_rows,
    key_rows,
    value_rows,
    out_grad,
    params,
    momentum,
    token_ids,
    block_mask,
    step_index,
):
    correction = 1.0 / (
        1.0 - jnp.exp((step_index[0] + 1).astype(jnp.float32) * math.log(MOMENTUM_RATE))
    )
    rate = (LEARN_RATE * correction).reshape(1)
    count = lax.axis_size("fsdp")
    me = lax.axis_index("fsdp")
    place = me.astype(jnp.int32).reshape(1)
    local, inner = params.shape[0], params.shape[0] * count
    route = partner_route(lax.axis_size("dp"), bit_level)
    shifts = range(1, count)
    near = bit_level == 0
    groups = math.gcd(local // HD, 2) if near else 1
    span = local // groups
    if near:
        chunks = [[(group * span, span)] for group in range(groups)]
    else:
        chunks = [row_chunks(group * span, span) for group in range(groups)]

    if not near:
        query_rows, key_rows, value_rows, out_grad = (
            in_hbm(rows) for rows in (query_rows, key_rows, value_rows, out_grad)
        )
    tensors = (query_rows, key_rows, value_rows)
    rings = [shift_route(count, shift) for shift in shifts]
    far_params = []
    read_params = params
    if not near:
        read_params = in_hbm(params)
        cut = chunks[0][-2][0] if len(chunks[0]) > 2 else local
        for start, size in ((0, cut), (cut, local - cut)):
            if size:
                short = short_rows(read_params, start, size)
                far_params.append((start, size, lax.ppermute(short, "dp", route)))

    packs, ids_sent = [], token_ids
    for group in range(groups):
        packs.append([])
        for shift, ring in zip(shifts, rings):
            pack, ids_copy = packed_heads(
                place, tensors, out_grad, token_ids, shift, count, group, groups
            )
            packs[group].append(lax.ppermute(pack, "fsdp", ring))
            if not near:
                ids_sent = ids_copy
    far_ids = [lax.ppermute(ids_sent, "fsdp", ring) for ring in rings]

    bias = score_bias(me, count, token_ids, far_ids, block_mask)
    attended, returned, results, grads = [], [], None, out_grad
    for group in range(groups):
        outs = attention_step(
            place,
            bias,
            tensors,
            packs[group],
            grads,
            read_params,
            results,
            count,
            group,
            groups,
            near,
        )
        attended.append(outs[0])
        results, backs = outs[1:4], outs[4 : 4 + len(shifts)]
        if group == 0:
            grads = outs[4 + len(shifts)]
        if near:
            far = lax.ppermute(outs[-1], "dp", route)
            far_params.append((group * span, span, far))
        returned.append(
            [
                lax.ppermute(back, "fsdp", shift_route(count, -shift))
                for shift, back in zip(shifts, backs)
            ]
        )
    sent = []
    for group in range(groups):
        gates = returned[0][:1] if group else []
        for start, size in chunks[group]:
            moment = moment_rows(
                attended[group], grads, momentum, start, size, group * span, inner, gates
            )
            sent.append((start, size, moment, lax.ppermute(moment, "dp", route)))
    means = None
    for start, size, moment, far_moment in sent:
        far_start, far = next(
            (first, rows) for first, many, rows in far_params if first <= start < first + many
        )
        means = averaged_rows(
            rate,
            params,
            far,
            far_start,
            moment,
            far_moment,
            start,
            size,
            means,
        )
    for group in range(groups):
        gates = means[:1] if group else []
        for shift, pack in zip(shifts, returned[group]):
            results = placed_heads(place, pack, results, shift, count, group, groups, gates)
    return (*results, *means)


def shards(
    query_rows, key_rows, value_rows, out_grad, params, momentum, token_ids, block_mask, step_index
):
    return lax.switch(
        step_index[0] & 3,
        [functools.partial(step_with_partner, bit_level) for bit_level in range(4)],
        query_rows,
        key_rows,
        value_rows,
        out_grad,
        params,
        momentum,
        token_ids,
        block_mask,
        step_index,
    )


def solution(mesh):
    rows = P(("dp", "fsdp"), None)
    return jax.shard_map(
        shards,
        mesh=mesh,
        in_specs=(rows,) * 6 + (P(("dp", "fsdp")), P(), P()),
        out_specs=(rows,) * 5,
        check_vma=False,
    )
```

```python
import functools
import math

import jax
import jax.numpy as jnp
from jax import lax
from jax.experimental import pallas as pl
from jax.experimental.pallas import tpu as pltpu
from jax.sharding import PartitionSpec as P

HD = 128
CODES = 2048
MOMENTUM_RATE = 0.9
LEARN_RATE = 0.25
MIB = 1 << 20

CONTRACT_LAST = (((1,), (1,)), ((), ()))
CONTRACT_FIRST = (((0,), (0,)), ((), ()))


def dot_f32(left, right, dims):
    return lax.dot_general(left, right, dims, preferred_element_type=jnp.float32)


def cost_of(macs, moved):
    return pl.CostEstimate(flops=2 * macs, bytes_accessed=moved, transcendentals=0)


def params_of(limit):
    return pltpu.CompilerParams(vmem_limit_bytes=limit)


def row_chunks(start, rows):
    units = rows // HD
    if units < 8:
        sizes = [1] * units
    else:
        part = units // 8
        sizes = [units - 4 * part, 2 * part, part, part]
    chunks = []
    for size in sizes:
        chunks.append((start, size * HD))
        start += size * HD
    return chunks


def in_hbm(array):
    return pltpu.with_memory_space_constraint(array, pltpu.HBM)


def partner_route(count, bit_level):
    route = []
    for low in range(count):
        high = low | 1 << bit_level
        if high != low and high < count:
            route += [(low, high), (high, low)]
    return route


def shift_route(count, shift):
    return [(source, (source + shift) % count) for source in range(count)]


def short_rows(params, start, size):
    width = params.shape[1]
    piece = math.gcd(size, HD)
    pieces = size // piece

    def body(wide_ref, short_ref, wide, in_sem):
        at = pl.program_id(0)

        def read(i):
            return pltpu.make_async_copy(
                wide_ref.at[pl.ds(start + i * piece, piece)], wide.at[i], in_sem.at[i]
            )

        @pl.when(at == 0)
        def _():
            for i in range(pieces):
                read(i).start()

        read(at).wait()
        short_ref[...] = wide[at].astype(jnp.bfloat16)

    return pl.pallas_call(
        body,
        grid=(pieces,),
        in_specs=[pl.BlockSpec(memory_space=pl.ANY)],
        out_specs=pl.BlockSpec((piece, width), lambda i: (i, 0)),
        out_shape=jax.ShapeDtypeStruct((size, width), jnp.bfloat16),
        scratch_shapes=[
            pltpu.VMEM((pieces, piece, width), jnp.float32),
            pltpu.SemaphoreType.DMA((pieces,)),
        ],
        compiler_params=params_of(4 * size * width + 4 * MIB),
        cost_estimate=cost_of(0, 6 * size * width),
        name="short_rows",
    )(params)


def packed_heads(place, gates, tensors, out_grad, token_ids, shift, count, group, groups):
    rows, width = tensors[0].shape
    span = width // count // groups
    slabs = out_grad.shape[1] // span if group == 0 else 0

    def body(place_ref, query_ref, key_ref, value_ref, *refs):
        pack_ref = refs[-2] if slabs else refs[-1]
        for slab in range(slabs):
            pack_ref[slab] = refs[0][:, slab * span : (slab + 1) * span]
        if slabs:
            refs[-1][...] = refs[1][...]
        pack_ref[slabs] = query_ref[...]
        pack_ref[slabs + 1] = key_ref[...]
        pack_ref[slabs + 2] = value_ref[...]

    spec = pl.BlockSpec(
        (rows, span),
        lambda i, place_ref: (0, lax.rem(place_ref[0] + shift, count) * groups + group),
    )
    grad_spec = pl.BlockSpec(out_grad.shape, lambda i, place_ref: (0, 0))
    ids_spec = pl.BlockSpec((1, rows), lambda i, place_ref: (0, 0))
    outs = pl.pallas_call(
        body,
        grid_spec=pltpu.PrefetchScalarGridSpec(
            num_scalar_prefetch=1,
            grid=(1,),
            in_specs=[spec] * 3
            + [grad_spec, ids_spec] * (slabs > 0)
            + [pl.BlockSpec(memory_space=pl.ANY)] * len(gates),
            out_specs=[
                pl.BlockSpec((slabs + 3, rows, span), lambda i, place_ref: (0, 0, 0))
            ]
            + [ids_spec] * (slabs > 0),
        ),
        out_shape=[jax.ShapeDtypeStruct((slabs + 3, rows, span), out_grad.dtype)]
        + [jax.ShapeDtypeStruct((1, rows), token_ids.dtype)] * (slabs > 0),
        compiler_params=params_of(12 * MIB),
        cost_estimate=cost_of(0, 4 * (slabs + 3) * rows * span),
        name="packed_heads",
    )(place, *tensors, *[out_grad, token_ids.reshape(1, rows)] * (slabs > 0), *gates)
    return outs[0], outs[1].reshape(rows) if slabs else None


def attention_step(
    place, bias, tensors, packs, grads, params, results, count, group, groups, short_out
):
    rows, width = tensors[0].shape
    tokens = rows * count
    heads = width // count // HD // groups
    together = math.gcd(heads, 2)
    span = together * HD
    steps = heads // together
    depth = params.shape[1]
    first = group == 0
    slabs = packs[0].shape[0] - 3 if packs else 0
    slab = heads * HD
    kept = [] if results is None else list(results)
    score_scale = 1.0 / math.sqrt(HD)
    inv_width = 1.0 / math.sqrt(width)
    far = count - 1

    def body(place_ref, bias_ref, query_ref, key_ref, value_ref, *refs):
        pack_refs, refs = [refs[3 * s : 3 * s + 3] for s in range(far)], refs[3 * far :]
        slab_refs, refs = refs[: far * first], refs[far * first :]
        grads_ref, params_ref = refs[:2]
        refs = refs[2 + len(kept) :]
        attended_ref, dq_ref, dk_ref, dv_ref = refs[:4]
        back_refs = refs[4 : 4 + far]

        if first:
            own_ref, grads_ref = grads_ref, refs[4 + far]

            @pl.when(pl.program_id(0) == 0)
            def _():
                grads_ref[:rows, :] = own_ref[...]
                for s in range(far):
                    for at in range(slabs):
                        grads_ref[
                            (s + 1) * rows : (s + 2) * rows, at * slab : (at + 1) * slab
                        ] = slab_refs[s][at]

        weight = params_ref[...].astype(jnp.bfloat16)
        if short_out:
            refs[-1][...] = weight
        grad_heads = (dot_f32(grads_ref[...], weight, CONTRACT_LAST) * inv_width).astype(
            jnp.bfloat16
        )
        for g in range(together):
            cols = slice(g * HD, (g + 1) * HD)

            def whole(own_ref, part):
                return jnp.concatenate(
                    [own_ref[:, cols]] + [far_refs[part][:, cols] for far_refs in pack_refs],
                    axis=0,
                )

            query, key, value = whole(query_ref, 0), whole(key_ref, 1), whole(value_ref, 2)
            grad = grad_heads[:, cols]
            scores = dot_f32(query, key, CONTRACT_LAST) * score_scale + bias_ref[...]
            top = jnp.max(scores, axis=-1, keepdims=True)
            terms = jnp.exp(scores - top)
            prob = terms * (1.0 / jnp.sum(terms, axis=-1, keepdims=True))
            prob16 = prob.astype(jnp.bfloat16)
            attended_ref[:, cols] = jnp.dot(
                prob16, value, preferred_element_type=jnp.float32
            ).astype(jnp.bfloat16)
            grad_value = dot_f32(prob16, grad, CONTRACT_FIRST).astype(jnp.bfloat16)
            grad_prob = dot_f32(grad, value, CONTRACT_LAST)
            row_dot = jnp.sum(prob * grad_prob, axis=-1, keepdims=True)
            grad_score = (prob * (grad_prob - row_dot) * score_scale).astype(jnp.bfloat16)
            grad_query = jnp.dot(
                grad_score, key, preferred_element_type=jnp.float32
            ).astype(jnp.bfloat16)
            grad_key = dot_f32(grad_score, query, CONTRACT_FIRST).astype(jnp.bfloat16)
            for part, (out_ref, result) in enumerate(
                ((dq_ref, grad_query), (dk_ref, grad_key), (dv_ref, grad_value))
            ):
                out_ref[:, cols] = result[:rows]
                for s in range(far):
                    back_refs[s][part, :, cols] = result[(s + 1) * rows : (s + 2) * rows]

    own_spec = pl.BlockSpec(
        (rows, span), lambda i, place_ref: (0, (place_ref[0] * groups + group) * steps + i)
    )
    pack_specs = [
        pl.BlockSpec((None, rows, span), lambda i, place_ref, part=part: (part, 0, i))
        for part in range(slabs, slabs + 3)
    ]
    back_spec = pl.BlockSpec((3, rows, span), lambda i, place_ref: (0, 0, i))
    all_spec = pl.BlockSpec((tokens, depth), lambda i, place_ref: (0, 0))
    own_shape = pltpu.HBM((rows, width), jnp.bfloat16)
    macs = tokens * depth * heads * HD + 5 * heads * tokens * tokens * HD
    operands = [place, bias, *tensors]
    for pack in packs:
        operands += [pack] * 3
    in_specs = (
        [pl.BlockSpec((tokens, tokens), lambda i, place_ref: (0, 0))]
        + [own_spec] * 3
        + pack_specs * far
    )
    if first:
        operands += packs
        in_specs += [
            pl.BlockSpec((slabs, rows, slab), lambda i, place_ref: (0, 0, 0))
        ] * far + [pl.BlockSpec((rows, depth), lambda i, place_ref: (0, 0))]
    else:
        in_specs += [all_spec]
    operands += [grads, params]
    in_specs += [pl.BlockSpec((span, depth), lambda i, place_ref: (group * steps + i, 0))]
    aliases = {len(operands) + i: 1 + i for i in range(len(kept))}
    in_specs += [pl.BlockSpec(memory_space=pl.ANY)] * len(kept)
    return pl.pallas_call(
        body,
        grid_spec=pltpu.PrefetchScalarGridSpec(
            num_scalar_prefetch=1,
            grid=(steps,),
            in_specs=in_specs,
            out_specs=[pl.BlockSpec((tokens, span), lambda i, place_ref: (0, i))]
            + [own_spec] * 3
            + [back_spec] * far
            + [all_spec] * first
            + [pl.BlockSpec((span, depth), lambda i, place_ref: (i, 0))] * short_out,
        ),
        out_shape=[jax.ShapeDtypeStruct((tokens, heads * HD), jnp.bfloat16)]
        + [own_shape] * 3
        + [jax.ShapeDtypeStruct((3, rows, heads * HD), jnp.bfloat16)] * far
        + [jax.ShapeDtypeStruct((tokens, depth), jnp.bfloat16)] * first
        + [jax.ShapeDtypeStruct((heads * HD, depth), jnp.bfloat16)] * short_out,
        input_output_aliases=aliases,
        compiler_params=params_of((24 if tokens <= 256 else 56) * MIB),
        cost_estimate=cost_of(macs, heads * HD * (4 * depth + 16 * tokens)),
        name="attention_step",
    )(*operands, *kept)


def moment_rows(attended, grads, momentum, start, size, group_start, inner, gates):
    tokens, depth = grads.shape
    step = math.gcd(size, 2 * HD)
    first = start // step
    first_column = (start - group_start) // step
    inv_width = 1.0 / math.sqrt(inner)


    def body(attended_ref, grads_ref, momentum_ref, *refs):
        total = dot_f32(attended_ref[...], grads_ref[...], CONTRACT_FIRST)
        refs[-1][...] = (
            MOMENTUM_RATE * momentum_ref[...] + total * inv_width
        ).astype(jnp.bfloat16)

    return pl.pallas_call(
        body,
        grid=(size // step,),
        in_specs=[
            pl.BlockSpec((tokens, step), lambda i: (0, first_column + i)),
            pl.BlockSpec((tokens, depth), lambda i: (0, 0)),
            pl.BlockSpec((step, depth), lambda i: (first + i, 0)),
        ]
        + [pl.BlockSpec(memory_space=pl.ANY)] * len(gates),
        out_specs=pl.BlockSpec((step, depth), lambda i: (i, 0)),
        out_shape=jax.ShapeDtypeStruct((size, depth), jnp.bfloat16),
        compiler_params=params_of(24 * MIB),
        cost_estimate=cost_of(
            tokens * size * depth, 6 * size * depth + 2 * tokens * depth
        ),
        name="moment_rows",
    )(attended, grads, momentum, *gates)


def averaged_rows(
    rate, params, far_params, far_start, moment, far_moment, start, size, results
):
    depth = params.shape[1]
    step = math.gcd(size, HD if size > HD else HD // 2)
    first = start // step
    far_first = (start - far_start) // step

    def body(rate_ref, params_ref, far_params_ref, moment_ref, far_moment_ref, *refs):
        new_params_ref, new_momentum_ref = refs[-2:]
        mean_moment = 0.5 * (
            moment_ref[...].astype(jnp.float32) + far_moment_ref[...].astype(jnp.float32)
        )
        mean_params = 0.5 * (params_ref[...] + far_params_ref[...].astype(jnp.float32))
        new_momentum_ref[...] = mean_moment
        new_params_ref[...] = mean_params - rate_ref[0] * mean_moment

    whole_spec = pl.BlockSpec((step, depth), lambda i: (first + i, 0))
    part_spec = pl.BlockSpec((step, depth), lambda i: (i, 0))
    kept = [] if results is None else list(results)
    return pl.pallas_call(
        body,
        grid=(size // step,),
        in_specs=[
            pl.BlockSpec(memory_space=pltpu.SMEM),
            whole_spec,
            pl.BlockSpec((step, depth), lambda i: (far_first + i, 0)),
            part_spec,
            part_spec,
        ]
        + [pl.BlockSpec(memory_space=pl.ANY)] * len(kept),
        out_specs=[whole_spec] * 2,
        out_shape=[pltpu.HBM(params.shape, jnp.float32)] * 2,
        input_output_aliases={5 + i: i for i in range(len(kept))},
        compiler_params=params_of(16 * MIB),
        cost_estimate=cost_of(3 * size * depth, 18 * size * depth),
        name="averaged_rows",
    )(rate, params, far_params, moment, far_moment, *kept)


def placed_heads(place, pack, results, shift, count, group, groups, gates):
    rows, width = results[0].shape
    span = width // count // groups

    def body(place_ref, pack_ref, *refs):
        for part in range(3):
            refs[len(refs) - 3 + part][...] = pack_ref[part]

    spec = pl.BlockSpec(
        (rows, span),
        lambda i, place_ref: (0, lax.rem(place_ref[0] + shift, count) * groups + group),
    )
    return pl.pallas_call(
        body,
        grid_spec=pltpu.PrefetchScalarGridSpec(
            num_scalar_prefetch=1,
            grid=(1,),
            in_specs=[pl.BlockSpec((3, rows, span), lambda i, place_ref: (0, 0, 0))]
            + [pl.BlockSpec(memory_space=pl.ANY)] * (3 + len(gates)),
            out_specs=[spec] * 3,
        ),
        out_shape=[pltpu.HBM((rows, width), jnp.bfloat16)] * 3,
        input_output_aliases={2 + part: part for part in range(3)},
        compiler_params=params_of(8 * MIB),
        cost_estimate=cost_of(0, 12 * rows * span),
        name="placed_heads",
    )(place, pack, *results, *gates)


def score_bias(me, count, own_ids, far_ids, block_mask):
    rows = own_ids.shape[0]
    blocks = block_mask.shape[0]
    block_rows = rows * count // blocks
    stems = jnp.concatenate([own_ids] + far_ids) // CODES
    position = jnp.concatenate(
        [lax.rem(me + count - s, count) * rows + jnp.arange(rows) for s in range(count)]
    )
    block_of = position // block_rows
    picks = (block_of[:, None] == jnp.arange(blocks)[None, :]).astype(jnp.float32)
    spread = jnp.dot(jnp.dot(picks, block_mask.astype(jnp.float32)), picks.T)
    allowed = (
        (spread > 0.5)
        & (position[None, :] <= position[:, None])
        & ((stems[:, None] == stems[None, :]) | (block_of[:, None] == block_of[None, :]))
    )
    return jnp.where(allowed, 0.0, -1e30)


def step_with_partner(
    bit_level,
    query_rows,
    key_rows,
    value_rows,
    out_grad,
    params,
    momentum,
    token_ids,
    block_mask,
    step_index,
):
    correction = 1.0 / (
        1.0 - jnp.exp((step_index[0] + 1).astype(jnp.float32) * math.log(MOMENTUM_RATE))
    )
    rate = (LEARN_RATE * correction).reshape(1)
    count = lax.axis_size("fsdp")
    me = lax.axis_index("fsdp")
    place = me.astype(jnp.int32).reshape(1)
    local, inner = params.shape[0], params.shape[0] * count
    route = partner_route(lax.axis_size("dp"), bit_level)
    shifts = range(1, count)
    near = bit_level == 0
    groups = math.gcd(local // HD, 2) if near else 1
    span = local // groups
    if near:
        chunks = [[(group * span, span)] for group in range(groups)]
    else:
        chunks = [row_chunks(group * span, span) for group in range(groups)]

    if not near:
        query_rows, key_rows, value_rows, out_grad = (
            in_hbm(rows) for rows in (query_rows, key_rows, value_rows, out_grad)
        )
    tensors = (query_rows, key_rows, value_rows)
    rings = [shift_route(count, shift) for shift in shifts]
    far_params, gates = [], []
    read_params = params
    if not near:
        read_params = in_hbm(params)
        cut, last = chunks[0][max(len(chunks[0]) - 2, 0)][0], chunks[0][-1][0]
        ranges = [(last, local - last), (0, cut), (cut, last - cut)]
        for start, size in ranges:
            if size:
                short = short_rows(read_params, start, size)
                far_params.append((start, size, lax.ppermute(short, "dp", route)))
        gates = [far_params[0][2]]

    packs, ids_sent = [], token_ids
    for group in range(groups):
        packs.append([])
        for shift, ring in zip(shifts, rings):
            pack, ids_copy = packed_heads(
                place, gates, tensors, out_grad, token_ids, shift, count, group, groups
            )
            packs[group].append(lax.ppermute(pack, "fsdp", ring))
            if not near:
                ids_sent = ids_copy
    far_ids = [lax.ppermute(ids_sent, "fsdp", ring) for ring in rings]

    bias = score_bias(me, count, token_ids, far_ids, block_mask)
    attended, returned, results, grads = [], [], None, out_grad
    for group in range(groups):
        outs = attention_step(
            place,
            bias,
            tensors,
            packs[group],
            grads,
            read_params,
            results,
            count,
            group,
            groups,
            near,
        )
        attended.append(outs[0])
        results, backs = outs[1:4], outs[4 : 4 + len(shifts)]
        if group == 0:
            grads = outs[4 + len(shifts)]
        if near:
            far = lax.ppermute(outs[-1], "dp", route)
            far_params.append((group * span, span, far))
        returned.append(
            [
                lax.ppermute(back, "fsdp", shift_route(count, -shift))
                for shift, back in zip(shifts, backs)
            ]
        )
    sent = []
    for group in range(groups):
        gates = returned[0][:1] if group else []
        for start, size in chunks[group]:
            moment = moment_rows(
                attended[group], grads, momentum, start, size, group * span, inner, gates
            )
            sent.append((start, size, moment, lax.ppermute(moment, "dp", route)))
    means = None
    for start, size, moment, far_moment in sent:
        far_start, far = next(
            (first, rows) for first, many, rows in far_params if first <= start < first + many
        )
        means = averaged_rows(
            rate,
            params,
            far,
            far_start,
            moment,
            far_moment,
            start,
            size,
            means,
        )
    for group in range(groups):
        gates = means[:1] if group else []
        for shift, pack in zip(shifts, returned[group]):
            results = placed_heads(place, pack, results, shift, count, group, groups, gates)
    return (*results, *means)


def shards(
    query_rows, key_rows, value_rows, out_grad, params, momentum, token_ids, block_mask, step_index
):
    return lax.switch(
        step_index[0] & 3,
        [functools.partial(step_with_partner, bit_level) for bit_level in range(4)],
        query_rows,
        key_rows,
        value_rows,
        out_grad,
        params,
        momentum,
        token_ids,
        block_mask,
        step_index,
    )


def solution(mesh):
    rows = P(("dp", "fsdp"), None)
    return jax.shard_map(
        shards,
        mesh=mesh,
        in_specs=(rows,) * 6 + (P(("dp", "fsdp")), P(), P()),
        out_specs=(rows,) * 5,
        check_vma=False,
    )
```
